256 devices in a mesh: dp: 16 (over z_hi, y), block: 16 (over z_lo, x, core).
Axes of the slice: x: 4, y: 4, z: 8 (z_hi: 4, z_lo: 2; z = z_hi * 2 + z_lo), core: 2. Of those that a mesh axis runs over, the one named last changes fastest.
Arguments:
- acts: bfloat16 [4096, 4608], P('dp', 'block'), may hold values from -6 to 6
- cotan: bfloat16 [4096, 32768], P('dp', 'block'), may hold values from -0.125 to 0.125
- sketch_basis: bfloat16 [16, 16, 256, 4608], P('block', 'dp'), may hold values from -0.09375 to 0.09375
- sketch_values: float32 [16, 16, 256], P('block', 'dp'), may hold values from 500 to 20000
- start_basis: bfloat16 [16, 16, 256, 4608], P('block', 'dp'), may hold values from -6 to 6
Outputs:
- new_basis: bfloat16 [16, 16, 256, 4608], P('block', 'dp')
- new_values: float32 [16, 16, 256], P('block', 'dp')
- update: bfloat16 [4608, 32768], P('dp', 'block')
The draws below stay inside these ranges and needn't reach their ends.
All inputs are finite; a program needn't handle non-finite values.
Results may differ from the reference program's by a relative error of at most 0.04.
Values may be sent and summed in bfloat16 or wider, within the bound.
A program may use at most 128 MiB of HBM per device.

```python
import math
import jax
import jax.numpy as jnp
from jax import lax

D = 4608
RANK = 256
BCOL = 128
ITERS = 2
TOK_DEV = 256
TOKENS = 4096
GROUPS = 16
OWNERS = 16
FFW = 32768


def with_spikes(array, stream_key, source, target, parts, factor):
    owner, partner = [(jnp.arange(array.shape[position]) // (array.shape[position] // parts)).reshape([-1 if axis == position else 1 for axis in range(array.ndim)]) for position in (source, target)]
    chosen = jax.random.permutation(stream_key, parts)[partner]
    strong = (owner == chosen) | (owner == (partner + parts // 2) % parts)
    return jnp.where(strong, factor * array, array)


def block_scale(stream_key, dims, cuts, least, top_value):
    def one(axis_at, parts):
        draws = jax.random.uniform(jax.random.fold_in(jax.random.fold_in(stream_key, 6), axis_at), (parts,), jnp.float32, least / len(cuts), top_value / len(cuts))
        return jnp.repeat(jnp.exp(draws), dims[axis_at] // parts).reshape((-1,) + (1,) * (len(dims) - axis_at - 1))

    level = one(*cuts[0])
    for cut in cuts[1:]:
        level = level * one(*cut)
    return level


def gaussian(stream_key, shape, spread, limit, split=(), kind=jnp.bfloat16):
    array = spread * jax.random.normal(stream_key, shape, jnp.float32)
    if split:
        array = array * block_scale(stream_key, shape, split, -0.22, 0.18)
    return jnp.clip(array, -limit, limit).astype(kind)


def bell_draw_with(stream_key, extent, deviation, reach, cuts, heavy, kind=jnp.bfloat16):
    entries = deviation * jax.random.normal(stream_key, extent, jnp.float32)
    if cuts:
        entries = entries * block_scale(stream_key, extent, cuts, -0.22, 0.18)
    return jnp.clip(with_spikes(entries, jax.random.fold_in(stream_key, 3), *heavy), -reach, reach).astype(kind)


def setup_inputs(seed: int = 0) -> dict:
    streams_of = jax.random.split(jax.random.key(seed), 6)
    return {
        "acts": gaussian(streams_of[0], (TOKENS, D), 1.0, 6.0, ((0, 16), (1, 16))),
        "cotan": bell_draw_with(streams_of[1], (TOKENS, FFW), TOKENS ** -0.5, 0.125, ((0, 16), (1, 16)), (0, 1, 16, 2.0)),
        "sketch_basis": gaussian(streams_of[2], (GROUPS, OWNERS, RANK, D), D ** -0.5, 0.09375, ((0, 16), (1, 16))),
        "sketch_values": jnp.clip(jnp.exp(math.log(20000.0) - 3.6888795 * jax.random.uniform(streams_of[3], (GROUPS, OWNERS, RANK), jnp.float32) ** block_scale(streams_of[3], (GROUPS, OWNERS, RANK), ((0, 16), (1, 16)), -0.2, 0.2)), 500.0, 20000.0),
        "start_basis": gaussian(streams_of[4], (GROUPS, OWNERS, RANK, D), 1.0, 6.0, ((0, 16), (1, 16))),
    }


epsilon = 1e-05

def sketch_block(grad_sum, basis, values, start_basis):
    grad_low = grad_sum.astype(jnp.bfloat16)
    scaled = (jnp.sqrt(values)[:, None] * basis.astype(jnp.float32)).astype(jnp.bfloat16)
    stacked = jnp.concatenate([scaled, grad_low], axis=0)
    rank_rows = basis.shape[0]
    basis_now = start_basis
    for sweep in range(ITERS):
        coords = lax.dot_general(basis_now.astype(jnp.float32), stacked.astype(jnp.float32), (((1,), (1,)), ((), ())), preferred_element_type=jnp.float32).astype(jnp.bfloat16)
        images = jnp.dot(coords.astype(jnp.float32), stacked.astype(jnp.float32), preferred_element_type=jnp.float32)
        gram_matrix = jnp.dot(images, images.T, precision=lax.Precision.HIGHEST)
        factor = jnp.linalg.cholesky(gram_matrix)
        basis_now = lax.linalg.triangular_solve(factor, images, left_side=True, lower=True).astype(jnp.bfloat16)
    final = lax.dot_general(basis_now.astype(jnp.float32), stacked.astype(jnp.float32), (((1,), (1,)), ((), ())), preferred_element_type=jnp.float32)
    energy = lax.optimization_barrier(jnp.sum(final * final, axis=1))
    lowest = jnp.min(energy)
    new_values = energy - lowest
    shrink = ((lowest + epsilon) / energy) ** 0.25 - 1.0
    weights = (shrink[:, None] * final[:, rank_rows:]).astype(jnp.bfloat16)
    return (basis_now, new_values, grad_low, weights)

def block_update(basis_now, grad_low, weights):
    projected = lax.dot_general(basis_now.astype(jnp.float32), weights.astype(jnp.float32), (((0,), (0,)), ((), ())), preferred_element_type=jnp.float32)
    return (grad_low.astype(jnp.float32).T + projected).astype(jnp.bfloat16)

def reference(acts, cotan, sketch_basis, sketch_values, start_basis):
    blocks = GROUPS * OWNERS
    acts_parts = acts.reshape(OWNERS, TOK_DEV, D).astype(jnp.float32)
    cot_parts = cotan.reshape(OWNERS, TOK_DEV, blocks, BCOL)
    basis_flat = sketch_basis.reshape(blocks, RANK, D)
    values_flat = sketch_values.reshape(blocks, RANK)
    start_flat = start_basis.reshape(blocks, RANK, D)

    def one_block(block_index):
        columns = lax.dynamic_index_in_dim(cot_parts, block_index, 2, keepdims=False).astype(jnp.float32)
        partials = jnp.einsum('stc,sti->sci', columns, acts_parts).astype(jnp.bfloat16)
        partials = lax.optimization_barrier(partials).astype(jnp.float32)
        grad_sum = lax.optimization_barrier(jnp.sum(partials, axis=0))
        basis_now, new_values, grad_low, weights = sketch_block(grad_sum, basis_flat[block_index], values_flat[block_index], start_flat[block_index])
        return (basis_now, new_values, block_update(basis_now, grad_low, weights))
    new_basis, new_values, updates = lax.map(one_block, jnp.arange(blocks, dtype=jnp.int32))
    update = jnp.transpose(updates, (1, 0, 2)).reshape(D, blocks * BCOL)
    return (new_basis.reshape(GROUPS, OWNERS, RANK, D), new_values.reshape(GROUPS, OWNERS, RANK), update)
```

```python
import functools

import jax
import jax.numpy as jnp
from jax import lax
from jax.experimental import pallas as pl
from jax.experimental.pallas import tpu as pltpu
from jax.sharding import PartitionSpec as P

HIGH = lax.Precision.HIGHEST
F32, BF = jnp.float32, jnp.bfloat16
EPSILON = 1e-05
MESH = pl.DeviceIdType.MESH
PANEL = 8


def mm(a, b, ca, cb, precision=None):
    return lax.dot_general(
        a, b, (((ca,), (cb,)), ((), ())), precision=precision, preferred_element_type=F32
    )


def split(value, parts=3):
    out = []
    for _ in range(parts):
        out.append(value.astype(BF))
        value = value - out[-1].astype(F32)
    return out


def inverse_factor(block):
    n = block.shape[0]
    count = n // 8
    rows = [block[8 * i : 8 * i + 8, :] for i in range(count)]
    lane = lax.broadcasted_iota(jnp.int32, (8, n), 1)
    sub = lax.broadcasted_iota(jnp.int32, (8, n), 0)

    def full(v):
        return jnp.broadcast_to(v, (8, n))

    for start in range(0, n, PANEL):
        first = start // 8
        cols = [
            {i: full(rows[i][:, start + q : start + q + 1]) for i in range(first, count)}
            for q in range(PANEL)
        ]
        for q in range(PANEL):
            j = start + q
            b, r = divmod(j, 8)
            recip = 1.0 / full(cols[q][b][r : r + 1, :])
            mine = {i: cols[q][i] for i in range(b, count)}
            if r == 7:
                del mine[b]
            else:
                mine[b] = jnp.where(sub > r, mine[b], 0.0)
            mine = {i: m * recip for i, m in mine.items()}
            for k in range(q + 1, PANEL):
                pivot = full(cols[k][b][r : r + 1, :])
                for i, m in mine.items():
                    cols[k][i] = cols[k][i] - m * pivot
            here = lane == j
            row = jnp.where(here, 1.0, full(rows[b][r : r + 1, :]))
            for i, m in mine.items():
                gone = here & (sub > r) if i == b else here
                rows[i] = jnp.where(gone, 0.0, rows[i]) - m * row
    m = jnp.concatenate(rows, axis=0)
    ln = lax.broadcasted_iota(jnp.int32, (n, n), 1)
    sb = lax.broadcasted_iota(jnp.int32, (n, n), 0)
    diag = jnp.sum(jnp.where(ln == sb, m, 0.0), axis=1, keepdims=True)
    low = jnp.where(sb > ln, m, jnp.where(sb == ln, 1.0, 0.0))
    return low * lax.rsqrt(diag)


def solver(gram):
    h = gram.shape[0] // 2
    top = inverse_factor(gram[:h, :h])
    side = mm(gram[h:, :h], top, 1, 1, HIGH)
    low = inverse_factor(gram[h:, h:] - mm(side, side, 1, 1, HIGH))

    def solve(x):
        head = mm(top, x[:h], 1, 0, HIGH)
        tail = mm(low, x[h:] - mm(side, head, 1, 0, HIGH), 1, 0, HIGH)
        return jnp.concatenate([head, tail], axis=0)

    return solve


def sketch_kernel(grad_ref, basis_ref, values_ref, start_ref, new_ref, energy_ref, update_ref, scaled_ref):
    rank, depth = basis_ref.shape
    width = grad_ref.shape[1]
    step = 512
    eye = lax.broadcasted_iota(jnp.int32, (rank, rank), 0) == lax.broadcasted_iota(
        jnp.int32, (rank, rank), 1
    )
    root = jnp.sqrt(jnp.sum(jnp.where(eye, values_ref[...], 0.0), axis=1, keepdims=True))

    gram_bb = jnp.zeros((rank, rank), F32)
    coord_b = jnp.zeros((rank, rank), F32)
    gram_bg = jnp.zeros((rank, width), F32)
    coord_g = jnp.zeros((rank, width), F32)
    gram_gg = jnp.zeros((width, width), F32)
    for at in range(0, depth, step):
        cut = slice(at, at + step)
        scaled = (root * basis_ref[:, cut].astype(F32)).astype(BF)
        scaled_ref[:, cut] = scaled
        start = start_ref[:, cut]
        grad = grad_ref[cut, :]
        gram_bb += mm(scaled, scaled, 1, 1)
        coord_b += mm(start, scaled, 1, 1)
        gram_bg += mm(scaled, grad, 1, 0)
        coord_g += mm(start, grad, 1, 0)
        gram_gg += mm(grad, grad, 0, 0)
    gram = jnp.concatenate(
        [
            jnp.concatenate([gram_bb, gram_bg], axis=1),
            jnp.concatenate([gram_bg.T, gram_gg], axis=1),
        ],
        axis=0,
    )
    gram_parts = split(gram)

    def sweep(coords):
        mapped = sum(mm(coords, part, 1, 0) for part in gram_parts)
        images_gram = sum(mm(part, coords, 1, 1) for part in split(mapped))
        return mapped, solver(images_gram)

    coords = jnp.concatenate([coord_b, coord_g], axis=1).astype(BF)
    mapped, solve = sweep(coords)
    coords = solve(mapped).astype(BF)
    mapped, solve = sweep(coords)
    total = coords.shape[1]
    solved = solve(jnp.concatenate([coords.astype(F32), mapped], axis=1))
    combine = split(solved[:, :total])
    final = solved[:, total:]
    square = final * final
    energy = jnp.sum(square, axis=1, keepdims=True)
    lowest = jnp.min(energy)
    energy_row = jnp.sum(jnp.where(eye, energy, 0.0), axis=0, keepdims=True)
    energy_ref[...] = energy_row - lowest
    shrink = jnp.sqrt(jnp.sqrt((lowest + EPSILON) / energy)) - 1.0
    weights = (shrink * final[:, rank:]).astype(BF)
    for at in range(0, depth, step):
        cut = slice(at, at + step)
        grad = grad_ref[cut, :]
        scaled = scaled_ref[:, cut]
        basis = sum(mm(part[:, :rank], scaled, 1, 0) for part in combine)
        basis += sum(mm(part[:, rank:], grad, 1, 1) for part in combine)
        basis = basis.astype(BF)
        new_ref[:, cut] = basis
        update_ref[cut, :] = (grad.astype(F32) + mm(basis, weights, 0, 0)).astype(BF)


def sketch(grad, basis, values, start):
    rank, depth = basis.shape
    width = grad.shape[1]
    vmem = pl.BlockSpec(memory_space=pltpu.VMEM)
    return pl.pallas_call(
        sketch_kernel,
        out_shape=(
            jax.ShapeDtypeStruct((rank, depth), BF),
            jax.ShapeDtypeStruct((1, rank), F32),
            jax.ShapeDtypeStruct((depth, width), BF),
        ),
        in_specs=[vmem] * 4,
        out_specs=(vmem, vmem, vmem),
        scratch_shapes=[pltpu.VMEM((rank, depth), BF)],
        compiler_params=pltpu.CompilerParams(vmem_limit_bytes=48 << 20),
    )(grad, basis, values, start)


def exchange_kernel(shares, update_ref, out_ref, own_sem, send_sem, recv_sem):
    zh, y = lax.axis_index("zh"), lax.axis_index("y")
    ys = lax.axis_size("y")
    me = zh * ys + y
    rows, width = out_ref.shape[0], update_ref.shape[1]
    peers = [lax.rem(me + r, shares) for r in range(shares)]

    barrier = pltpu.get_barrier_semaphore()
    for peer in peers[1:]:
        pl.semaphore_signal(
            barrier, inc=1, device_id={"zh": peer // ys, "y": lax.rem(peer, ys)}, device_id_type=MESH
        )
    pl.semaphore_wait(barrier, shares - 1)

    columns = out_ref.at[:, pl.ds(pl.multiple_of(me * width, width), width)]

    def piece(peer):
        return update_ref.at[pl.ds(pl.multiple_of(peer * rows, 16), rows), :]

    copies = []
    for r in range(1, shares):
        peer = peers[r]
        copy = pltpu.make_async_remote_copy(
            src_ref=piece(peer),
            dst_ref=columns,
            send_sem=send_sem.at[r],
            recv_sem=recv_sem.at[r],
            device_id={"zh": peer // ys, "y": lax.rem(peer, ys)},
            device_id_type=MESH,
        )
        copy.start()
        copies.append(copy)
    own = pltpu.make_async_copy(piece(me), columns, own_sem)
    own.start()
    own.wait()
    for copy in copies:
        copy.wait()


def exchange(update, shares):
    depth, width = update.shape
    anywhere = pl.BlockSpec(memory_space=pl.ANY)
    return pl.pallas_call(
        functools.partial(exchange_kernel, shares),
        out_shape=jax.ShapeDtypeStruct((depth // shares, width * shares), BF),
        in_specs=[anywhere],
        out_specs=anywhere,
        scratch_shapes=[
            pltpu.SemaphoreType.DMA,
            pltpu.SemaphoreType.DMA((shares,)),
            pltpu.SemaphoreType.DMA((shares,)),
        ],
        compiler_params=pltpu.CompilerParams(collective_id=1, has_side_effects=True),
    )(update)


def per_device(acts, cotan, sketch_basis, sketch_values, start_basis):
    gathered = lax.all_gather(acts, ("zl", "x", "c"), axis=1, tiled=True)
    shares = lax.axis_size("zh") * lax.axis_size("y")
    grad = lax.psum_scatter(
        lax.dot_general(
            cotan, gathered, (((0,), (0,)), ((), ())), preferred_element_type=F32
        ).astype(BF),
        ("zh", "y"),
        scatter_dimension=0,
        tiled=True,
    ).T
    basis, values, update = sketch(grad, sketch_basis[0, 0], sketch_values[0], start_basis[0, 0])
    update = exchange(update, shares)
    return basis[None, None], values[None], update


def solution(mesh):
    fine = jax.sharding.Mesh(mesh.devices.reshape(4, 4, 2, 4, 2), ("zh", "y", "zl", "x", "c"))
    dp, block = ("zh", "y"), ("zl", "x", "c")
    return jax.shard_map(
        per_device,
        mesh=fine,
        in_specs=(
            P(dp, block),
            P(dp, block),
            P(block, dp, None, None),
            P(block, dp, None),
            P(block, dp, None, None),
        ),
        out_specs=(P(block, dp, None, None), P(block, dp, None), P(dp, block)),
        check_vma=False,
    )
```

```python
import functools

import jax
import jax.numpy as jnp
from jax import lax
from jax.experimental import pallas as pl
from jax.experimental.pallas import tpu as pltpu
from jax.sharding import PartitionSpec as P

HIGH = lax.Precision.HIGHEST
F32, BF = jnp.float32, jnp.bfloat16
EPSILON = 1e-05
MESH = pl.DeviceIdType.MESH
PANEL = 8


def mm(a, b, ca, cb, precision=None):
    return lax.dot_general(
        a, b, (((ca,), (cb,)), ((), ())), precision=precision, preferred_element_type=F32
    )


def split(value, parts=3):
    out = []
    for _ in range(parts):
        out.append(value.astype(BF))
        value = value - out[-1].astype(F32)
    return out


def inverse_factor(block):
    n = block.shape[0]
    count = n // 8
    rows = [block[8 * i : 8 * i + 8, :] for i in range(count)]
    lane = lax.broadcasted_iota(jnp.int32, (8, n), 1)
    sub = lax.broadcasted_iota(jnp.int32, (8, n), 0)

    def full(v):
        return jnp.broadcast_to(v, (8, n))

    for start in range(0, n, PANEL):
        first = start // 8
        cols = [
            {i: full(rows[i][:, start + q : start + q + 1]) for i in range(first, count)}
            for q in range(PANEL)
        ]
        for q in range(PANEL):
            j = start + q
            b, r = divmod(j, 8)
            recip = 1.0 / full(cols[q][b][r : r + 1, :])
            mine = {i: cols[q][i] for i in range(b, count)}
            if r == 7:
                del mine[b]
            else:
                mine[b] = jnp.where(sub > r, mine[b], 0.0)
            mine = {i: m * recip for i, m in mine.items()}
            for k in range(q + 1, PANEL):
                pivot = full(cols[k][b][r : r + 1, :])
                for i, m in mine.items():
                    cols[k][i] = cols[k][i] - m * pivot
            here = lane == j
            row = jnp.where(here, 1.0, full(rows[b][r : r + 1, :]))
            for i, m in mine.items():
                gone = here & (sub > r) if i == b else here
                rows[i] = jnp.where(gone, 0.0, rows[i]) - m * row
    m = jnp.concatenate(rows, axis=0)
    ln = lax.broadcasted_iota(jnp.int32, (n, n), 1)
    sb = lax.broadcasted_iota(jnp.int32, (n, n), 0)
    diag = jnp.sum(jnp.where(ln == sb, m, 0.0), axis=1, keepdims=True)
    low = jnp.where(sb > ln, m, jnp.where(sb == ln, 1.0, 0.0))
    return low * lax.rsqrt(diag)


def solver(gram):
    h = gram.shape[0] // 2
    top = inverse_factor(gram[:h, :h])
    side = mm(gram[h:, :h], top, 1, 1, HIGH)
    low = inverse_factor(gram[h:, h:] - mm(side, side, 1, 1, HIGH))

    def solve(x):
        head = mm(top, x[:h], 1, 0, HIGH)
        tail = mm(low, x[h:] - mm(side, head, 1, 0, HIGH), 1, 0, HIGH)
        return jnp.concatenate([head, tail], axis=0)

    return solve


def sketch_kernel(grad_ref, basis_ref, values_ref, start_ref, new_ref, energy_ref, update_ref, scaled_ref):
    rank, depth = basis_ref.shape
    width = grad_ref.shape[1]
    step = 512
    eye = lax.broadcasted_iota(jnp.int32, (rank, rank), 0) == lax.broadcasted_iota(
        jnp.int32, (rank, rank), 1
    )
    root = jnp.sqrt(jnp.sum(jnp.where(eye, values_ref[...], 0.0), axis=1, keepdims=True))

    gram_bb = jnp.zeros((rank, rank), F32)
    coord_b = jnp.zeros((rank, rank), F32)
    gram_bg = jnp.zeros((rank, width), F32)
    coord_g = jnp.zeros((rank, width), F32)
    gram_gg = jnp.zeros((width, width), F32)
    for at in range(0, depth, step):
        cut = slice(at, at + step)
        scaled = (root * basis_ref[:, cut].astype(F32)).astype(BF)
        scaled_ref[:, cut] = scaled
        start = start_ref[:, cut]
        grad = grad_ref[cut, :]
        gram_bb += mm(scaled, scaled, 1, 1)
        coord_b += mm(start, scaled, 1, 1)
        gram_bg += mm(scaled, grad, 1, 0)
        coord_g += mm(start, grad, 1, 0)
        gram_gg += mm(grad, grad, 0, 0)
    gram = jnp.concatenate(
        [
            jnp.concatenate([gram_bb, gram_bg], axis=1),
            jnp.concatenate([gram_bg.T, gram_gg], axis=1),
        ],
        axis=0,
    )
    gram_parts = split(gram)

    def sweep(coords):
        mapped = sum(mm(coords, part, 1, 0) for part in gram_parts)
        images_gram = sum(mm(part, coords, 1, 1) for part in split(mapped))
        return mapped, solver(images_gram)

    coords = jnp.concatenate([coord_b, coord_g], axis=1).astype(BF)
    mapped, solve = sweep(coords)
    coords = solve(mapped).astype(BF)
    mapped, solve = sweep(coords)
    total = coords.shape[1]
    solved = solve(jnp.concatenate([coords.astype(F32), mapped], axis=1))
    combine = split(solved[:, :total])
    final = solved[:, total:]
    square = final * final
    energy = jnp.sum(square, axis=1, keepdims=True)
    lowest = jnp.min(energy)
    energy_row = jnp.sum(jnp.where(eye, energy, 0.0), axis=0, keepdims=True)
    energy_ref[...] = energy_row - lowest
    shrink = jnp.sqrt(jnp.sqrt((lowest + EPSILON) / energy)) - 1.0
    weights = (shrink * final[:, rank:]).astype(BF)
    for at in range(0, depth, step):
        cut = slice(at, at + step)
        grad = grad_ref[cut, :]
        scaled = scaled_ref[:, cut]
        basis = sum(mm(part[:, :rank], scaled, 1, 0) for part in combine)
        basis += sum(mm(part[:, rank:], grad, 1, 1) for part in combine)
        basis = basis.astype(BF)
        new_ref[:, cut] = basis
        update_ref[cut, :] = (grad.astype(F32) + mm(basis, weights, 0, 0)).astype(BF)


def sketch(grad, basis, values, start):
    rank, depth = basis.shape
    width = grad.shape[1]
    vmem = pl.BlockSpec(memory_space=pltpu.VMEM)
    return pl.pallas_call(
        sketch_kernel,
        out_shape=(
            jax.ShapeDtypeStruct((rank, depth), BF),
            jax.ShapeDtypeStruct((1, rank), F32),
            jax.ShapeDtypeStruct((depth, width), BF),
        ),
        in_specs=[vmem] * 4,
        out_specs=(vmem, vmem, vmem),
        scratch_shapes=[pltpu.VMEM((rank, depth), BF)],
        compiler_params=pltpu.CompilerParams(vmem_limit_bytes=48 << 20),
    )(grad, basis, values, start)


def exchange_kernel(shares, update_ref, out_ref, own_sem, send_sem, recv_sem):
    zh, y = lax.axis_index("zh"), lax.axis_index("y")
    ys = lax.axis_size("y")
    me = zh * ys + y
    rows, width = out_ref.shape[0], update_ref.shape[1]
    peers = [lax.rem(me + r, shares) for r in range(shares)]

    barrier = pltpu.get_barrier_semaphore()
    for peer in peers[1:]:
        pl.semaphore_signal(
            barrier, inc=1, device_id={"zh": peer // ys, "y": lax.rem(peer, ys)}, device_id_type=MESH
        )
    pl.semaphore_wait(barrier, shares - 1)

    columns = out_ref.at[:, pl.ds(pl.multiple_of(me * width, width), width)]

    def piece(peer):
        return update_ref.at[pl.ds(pl.multiple_of(peer * rows, 16), rows), :]

    copies = []
    for r in range(1, shares):
        peer = peers[r]
        copy = pltpu.make_async_remote_copy(
            src_ref=piece(peer),
            dst_ref=columns,
            send_sem=send_sem.at[r],
            recv_sem=recv_sem.at[r],
            device_id={"zh": peer // ys, "y": lax.rem(peer, ys)},
            device_id_type=MESH,
        )
        copy.start()
        copies.append(copy)
    own = pltpu.make_async_copy(piece(me), columns, own_sem)
    own.start()
    own.wait()
    for copy in copies:
        copy.wait()


def exchange(update, shares):
    depth, width = update.shape
    anywhere = pl.BlockSpec(memory_space=pl.ANY)
    return pl.pallas_call(
        functools.partial(exchange_kernel, shares),
        out_shape=jax.ShapeDtypeStruct((depth // shares, width * shares), BF),
        in_specs=[anywhere],
        out_specs=anywhere,
        scratch_shapes=[
            pltpu.SemaphoreType.DMA,
            pltpu.SemaphoreType.DMA((shares,)),
            pltpu.SemaphoreType.DMA((shares,)),
        ],
        compiler_params=pltpu.CompilerParams(collective_id=1, has_side_effects=True),
    )(update)


def gradient_kernel(
    acts_ref, cotan_ref, out_ref, acts_all, cotan_all, total, sums,
    own_sem, z_send, z_recv, y_send, y_recv, d_send, d_recv, x_send, x_recv, c_send, c_recv, g_send, g_recv,
):
    zh, y, zl, x, c = (lax.axis_index(name) for name in ("zh", "y", "zl", "x", "c"))
    feats, tokens = acts_ref.shape
    width = out_ref.shape[-1]

    def ring(value, shift):
        return lax.rem(value + shift, 4)

    def remote(src, dst, send, recv, **where):
        return pltpu.make_async_remote_copy(
            src_ref=src, dst_ref=dst, send_sem=send, recv_sem=recv, device_id=where, device_id_type=MESH
        )

    barrier = pltpu.get_barrier_semaphore()
    greeted = 0
    for i in range(4):
        for j in range(4):
            if i or j:
                pl.semaphore_signal(
                    barrier, inc=1, device_id={"zh": ring(zh, i), "y": ring(y, j)}, device_id_type=MESH
                )
                greeted += 1
        pl.semaphore_signal(
            barrier, inc=1, device_id={"zh": ring(zh, i), "zl": 1 - zl}, device_id_type=MESH
        )
        greeted += 1
        for flip in range(2):
            if i or flip:
                pl.semaphore_signal(
                    barrier,
                    inc=1,
                    device_id={"x": ring(x, i), "c": lax.rem(c + flip, 2)},
                    device_id_type=MESH,
                )
                greeted += 1
    pl.semaphore_wait(barrier, greeted)

    started = []

    def go(copy):
        copy.start()
        started.append(copy)

    def column(xx, cc):
        return pl.ds(pl.multiple_of((xx * 2 + cc) * width, width), width)

    mine = column(x, c)
    order = (0, 1, 3, 2)

    def z_copy(to_zh, to_zl):
        return remote(
            acts_ref, acts_all.at[y, zh, zl], z_send.at[to_zh * 2 + to_zl], z_recv.at[zh * 2 + zl],
            zh=to_zh, zl=to_zl,
        )

    def d_copy(to_zh, to_y):
        piece = pl.ds(pl.multiple_of((to_zh * 4 + to_y) * width, width), width)
        return remote(
            cotan_ref.at[:, piece], cotan_all.at[zh, y, :, mine],
            d_send.at[to_zh * 4 + to_y], d_recv.at[zh * 4 + y], zh=to_zh, y=to_y,
        )

    for r in order:
        if r:
            go(z_copy(ring(zh, r), zl))
        go(z_copy(ring(zh, r), 1 - zl))
        for j in order:
            if r or j:
                go(d_copy(ring(zh, r), ring(y, j)))
    own_acts = pltpu.make_async_copy(acts_ref, acts_all.at[y, zh, zl], own_sem.at[0])
    own_acts.start()
    piece = pl.ds(pl.multiple_of((zh * 4 + y) * width, width), width)
    own_cotan = pltpu.make_async_copy(cotan_ref.at[:, piece], cotan_all.at[zh, y, :, mine], own_sem.at[1])
    own_cotan.start()

    def arrived(dst, sem):
        remote(dst, dst, sem, sem, x=ring(x, 1)).wait_recv()

    def first(t):
        r = order[t]
        src = ring(zh, r)
        if r:
            arrived(acts_all.at[y, src, zl], z_recv.at[src * 2 + zl])
        else:
            own_acts.wait()
        arrived(acts_all.at[y, src, 1 - zl], z_recv.at[src * 2 + 1 - zl])
        block = acts_all.at[y, src]
        go(remote(block, block, y_send.at[0, src], y_recv.at[0, src], y=ring(y, 1)))
        go(remote(block, block, y_send.at[1, src], y_recv.at[1, src], y=ring(y, 3)))
        for j in range(4):
            if r or j:
                yy = ring(y, j)
                arrived(cotan_all.at[src, yy, :, mine], d_recv.at[src * 4 + yy])
            else:
                own_cotan.wait()
        block = cotan_all.at[src, :, :, mine]
        go(remote(block, block, x_send.at[0, src], x_recv.at[0, src], x=ring(x, 1)))
        go(remote(block, block, x_send.at[1, src], x_recv.at[1, src], x=ring(x, 3)))
        go(remote(block, block, c_send.at[0, src], c_recv.at[0, src], c=1 - c))

    def second(t):
        src = ring(zh, order[t])
        up = t % 2 == 0
        for k, (shift, onward) in enumerate(((3, up), (1, not up))):
            block = acts_all.at[ring(y, shift), src]
            arrived(block, y_recv.at[k, src])
            if onward:
                go(remote(block, block, y_send.at[2, src], y_recv.at[2, src], y=ring(y, 4 - shift)))
        for k, (shift, onward) in enumerate(((3, up), (1, not up))):
            block = cotan_all.at[src, :, :, column(ring(x, shift), c)]
            arrived(block, x_recv.at[k, src])
            if onward:
                go(remote(block, block, x_send.at[2, src], x_recv.at[2, src], x=ring(x, 4 - shift)))
            go(remote(block, block, c_send.at[shift, src], c_recv.at[shift, src], c=1 - c))

    def third(t):
        src = ring(zh, order[t])
        block = cotan_all.at[src, :, :, column(ring(x, 2), c)]
        arrived(block, x_recv.at[2, src])
        go(remote(block, block, c_send.at[2, src], c_recv.at[2, src], c=1 - c))
        arrived(acts_all.at[ring(y, 2), src], y_recv.at[2, src])

    def multiply(t):
        src = ring(zh, order[t])
        for shift in range(4):
            arrived(cotan_all.at[src, :, :, column(ring(x, shift), 1 - c)], c_recv.at[shift, src])

        def tile(n, carry):
            cut = pl.ds(pl.multiple_of(n * 256, 256), 256)
            part = jnp.zeros((2 * feats, 256), F32) if t == 0 else total[:, cut]
            for j in range(4):
                left = acts_all[j, src].reshape(2 * feats, tokens)
                part += mm(left, cotan_all[src, j, :, cut], 1, 0)
            if t == 3:
                sums[:, :, cut] = part.reshape(2, feats, 256).astype(BF)
            else:
                total[:, cut] = part
            return carry

        lax.fori_loop(0, 8 * width // 256, tile, 0)

    for t in range(7):
        if t < 4:
            first(t)
        if 0 <= t - 1 < 4:
            second(t - 1)
        if 0 <= t - 2 < 4:
            third(t - 2)
        if 0 <= t - 3 < 4:
            multiply(t - 3)

    own = pltpu.make_async_copy(sums.at[:, :, mine], out_ref.at[:, x * 2 + c], own_sem.at[2])
    own.start()
    for i in (2, 1, 3, 0):
        for flip in (0, 1):
            if i or flip:
                xx, cc = ring(x, i), lax.rem(c + flip, 2)
                go(
                    remote(
                        sums.at[:, :, column(xx, cc)], out_ref.at[:, x * 2 + c],
                        g_send.at[xx * 2 + cc], g_recv.at[x * 2 + c], x=xx, c=cc,
                    )
                )
    for i in range(4):
        for flip in range(2):
            if i or flip:
                at = ring(x, i) * 2 + lax.rem(c + flip, 2)
                arrived(out_ref.at[:, at], g_recv.at[at])
    own.wait()
    for copy in started:
        copy.wait_send()


def gradient(acts, cotan, width):
    feats, tokens = acts.shape
    dma = pltpu.SemaphoreType.DMA
    anywhere = pl.BlockSpec(memory_space=pl.ANY)
    return pl.pallas_call(
        gradient_kernel,
        out_shape=jax.ShapeDtypeStruct((2, 8, feats, width), BF),
        in_specs=[anywhere, anywhere],
        out_specs=anywhere,
        scratch_shapes=[
            pltpu.VMEM((4, 4, 2, feats, tokens), BF),
            pltpu.VMEM((4, 4, tokens, 8 * width), BF),
            pltpu.VMEM((2 * feats, 8 * width), F32),
            pltpu.VMEM((2, feats, 8 * width), BF),
            dma((3,)),
            dma((8,)), dma((8,)),
            dma((3, 4)), dma((3, 4)),
            dma((16,)), dma((16,)),
            dma((3, 4)), dma((3, 4)),
            dma((4, 4)), dma((4, 4)),
            dma((8,)), dma((8,)),
        ],
        compiler_params=pltpu.CompilerParams(
            collective_id=0, has_side_effects=True, vmem_limit_bytes=48 << 20
        ),
    )(acts, cotan)


def per_device(acts, cotan, sketch_basis, sketch_values, start_basis):
    shares = lax.axis_size("zh") * lax.axis_size("y")
    width = cotan.shape[1] // shares
    grad = gradient(acts.T, cotan, width).reshape(-1, width)
    basis, values, update = sketch(grad, sketch_basis[0, 0], sketch_values[0], start_basis[0, 0])
    update = exchange(update, shares)
    return basis[None, None], values[None], update


def solution(mesh):
    fine = jax.sharding.Mesh(mesh.devices.reshape(4, 4, 2, 4, 2), ("zh", "y", "zl", "x", "c"))
    dp, block = ("zh", "y"), ("zl", "x", "c")
    return jax.shard_map(
        per_device,
        mesh=fine,
        in_specs=(
            P(dp, block),
            P(dp, block),
            P(block, dp, None, None),
            P(block, dp, None),
            P(block, dp, None, None),
        ),
        out_specs=(P(block, dp, None, None), P(block, dp, None), P(dp, block)),
        check_vma=False,
    )
```

```python
import functools

import jax
import jax.numpy as jnp
from jax import lax
from jax.experimental import pallas as pl
from jax.experimental.pallas import tpu as pltpu
from jax.sharding import PartitionSpec as P

HIGH = lax.Precision.HIGHEST
F32, BF = jnp.float32, jnp.bfloat16
EPSILON = 1e-05
VMEM_LIMIT = 60 << 20
MESH = pl.DeviceIdType.MESH
PANEL = 8


def mm(a, b, ca, cb, precision=None):
    return lax.dot_general(
        a, b, (((ca,), (cb,)), ((), ())), precision=precision, preferred_element_type=F32
    )


def split(value, parts=3):
    out = []
    for _ in range(parts):
        out.append(value.astype(BF))
        value = value - out[-1].astype(F32)
    return out


def inverse_factor(block):
    n = block.shape[0]
    count = n // 8
    rows = [block[8 * i : 8 * i + 8, :] for i in range(count)]
    lane = lax.broadcasted_iota(jnp.int32, (8, n), 1)
    sub = lax.broadcasted_iota(jnp.int32, (8, n), 0)

    def full(v):
        return jnp.broadcast_to(v, (8, n))

    for start in range(0, n, PANEL):
        first = start // 8
        cols = [
            {i: full(rows[i][:, start + q : start + q + 1]) for i in range(first, count)}
            for q in range(PANEL)
        ]
        for q in range(PANEL):
            j = start + q
            b, r = divmod(j, 8)
            recip = 1.0 / full(cols[q][b][r : r + 1, :])
            mine = {i: cols[q][i] for i in range(b, count)}
            if r == 7:
                del mine[b]
            else:
                mine[b] = jnp.where(sub > r, mine[b], 0.0)
            mine = {i: m * recip for i, m in mine.items()}
            for k in range(q + 1, PANEL):
                pivot = full(cols[k][b][r : r + 1, :])
                for i, m in mine.items():
                    cols[k][i] = cols[k][i] - m * pivot
            here = lane == j
            row = jnp.where(here, 1.0, full(rows[b][r : r + 1, :]))
            for i, m in mine.items():
                gone = here & (sub > r) if i == b else here
                rows[i] = jnp.where(gone, 0.0, rows[i]) - m * row
    m = jnp.concatenate(rows, axis=0)
    ln = lax.broadcasted_iota(jnp.int32, (n, n), 1)
    sb = lax.broadcasted_iota(jnp.int32, (n, n), 0)
    diag = jnp.sum(jnp.where(ln == sb, m, 0.0), axis=1, keepdims=True)
    low = jnp.where(sb > ln, m, jnp.where(sb == ln, 1.0, 0.0))
    return low * lax.rsqrt(diag)


def solver(gram):
    h = gram.shape[0] // 2
    top = inverse_factor(gram[:h, :h])
    side = mm(gram[h:, :h], top, 1, 1, HIGH)
    low = inverse_factor(gram[h:, h:] - mm(side, side, 1, 1, HIGH))

    def solve(x):
        head = mm(top, x[:h], 1, 0, HIGH)
        tail = mm(low, x[h:] - mm(side, head, 1, 0, HIGH), 1, 0, HIGH)
        return jnp.concatenate([head, tail], axis=0)

    return solve


def sketch_kernel(grad_ref, scaled_ref, gram_ref, coords_ref, new_ref, energy_ref, update_ref):
    rank, depth = scaled_ref.shape
    step = 512
    eye = lax.broadcasted_iota(jnp.int32, (rank, rank), 0) == lax.broadcasted_iota(
        jnp.int32, (rank, rank), 1
    )
    gram_parts = split(gram_ref[...])

    def sweep(coords):
        mapped = sum(mm(coords, part, 1, 0) for part in gram_parts)
        images_gram = sum(mm(part, coords, 1, 1) for part in split(mapped))
        return mapped, solver(images_gram)

    mapped, solve = sweep(coords_ref[...])
    coords = solve(mapped).astype(BF)
    mapped, solve = sweep(coords)
    total = coords.shape[1]
    solved = solve(jnp.concatenate([coords.astype(F32), mapped], axis=1))
    combine = split(solved[:, :total])
    final = solved[:, total:]
    square = final * final
    energy = jnp.sum(square, axis=1, keepdims=True)
    lowest = jnp.min(energy)
    energy_row = jnp.sum(jnp.where(eye, energy, 0.0), axis=0, keepdims=True)
    energy_ref[...] = energy_row - lowest
    shrink = jnp.sqrt(jnp.sqrt((lowest + EPSILON) / energy)) - 1.0
    weights = (shrink * final[:, rank:]).astype(BF)
    for at in range(0, depth, step):
        cut = slice(at, at + step)
        grad = grad_ref[cut, :]
        scaled = scaled_ref[:, cut]
        basis = sum(mm(part[:, :rank], scaled, 1, 0) for part in combine)
        basis += sum(mm(part[:, rank:], grad, 1, 1) for part in combine)
        basis = basis.astype(BF)
        new_ref[:, cut] = basis
        update_ref[cut, :] = (grad.astype(F32) + mm(basis, weights, 0, 0)).astype(BF)


def sketch(grad, scaled, gram, coords):
    rank, depth = scaled.shape
    width = grad.shape[1]
    vmem = pl.BlockSpec(memory_space=pltpu.VMEM)
    return pl.pallas_call(
        sketch_kernel,
        out_shape=(
            jax.ShapeDtypeStruct((rank, depth), BF),
            jax.ShapeDtypeStruct((1, rank), F32),
            jax.ShapeDtypeStruct((depth, width), BF),
        ),
        in_specs=[vmem] * 4,
        out_specs=(vmem, vmem, vmem),
        compiler_params=pltpu.CompilerParams(vmem_limit_bytes=VMEM_LIMIT),
    )(grad, scaled, gram, coords)


def exchange_kernel(shares, update_ref, out_ref, own_sem, send_sem, recv_sem):
    zh, y = lax.axis_index("zh"), lax.axis_index("y")
    ys = lax.axis_size("y")
    me = zh * ys + y
    rows, width = out_ref.shape[0], update_ref.shape[1]
    peers = [lax.rem(me + r, shares) for r in range(shares)]

    barrier = pltpu.get_barrier_semaphore()
    for peer in peers[1:]:
        pl.semaphore_signal(
            barrier, inc=1, device_id={"zh": peer // ys, "y": lax.rem(peer, ys)}, device_id_type=MESH
        )
    pl.semaphore_wait(barrier, shares - 1)

    columns = out_ref.at[:, pl.ds(pl.multiple_of(me * width, width), width)]

    def piece(peer):
        return update_ref.at[pl.ds(pl.multiple_of(peer * rows, 16), rows), :]

    copies = []
    for r in range(1, shares):
        peer = peers[r]
        copy = pltpu.make_async_remote_copy(
            src_ref=piece(peer),
            dst_ref=columns,
            send_sem=send_sem.at[r],
            recv_sem=recv_sem.at[r],
            device_id={"zh": peer // ys, "y": lax.rem(peer, ys)},
            device_id_type=MESH,
        )
        copy.start()
        copies.append(copy)
    own = pltpu.make_async_copy(piece(me), columns, own_sem)
    own.start()
    own.wait()
    for copy in copies:
        copy.wait()


def exchange(update, shares):
    depth, width = update.shape
    anywhere = pl.BlockSpec(memory_space=pl.ANY)
    return pl.pallas_call(
        functools.partial(exchange_kernel, shares),
        out_shape=jax.ShapeDtypeStruct((depth // shares, width * shares), BF),
        in_specs=[anywhere],
        out_specs=anywhere,
        scratch_shapes=[
            pltpu.SemaphoreType.DMA,
            pltpu.SemaphoreType.DMA((shares,)),
            pltpu.SemaphoreType.DMA((shares,)),
        ],
        compiler_params=pltpu.CompilerParams(
            collective_id=1, has_side_effects=True, vmem_limit_bytes=VMEM_LIMIT
        ),
    )(update)


def gradient_kernel(
    acts_ref, cotan_ref, basis_ref, values_ref, start_ref, grad_out, scaled_out, gram_ref, coords_ref,
    acts_all, cotan_all, total, sums, grad_ref, basis_in, start_in, gram_bb, coord_b,
    own_sem, z_send, z_recv, y_send, y_recv, d_send, d_recv, x_send, x_recv,
    c_send, c_recv, g_send, g_recv,
):
    zh, y, zl, x, c = (lax.axis_index(name) for name in ("zh", "y", "zl", "x", "c"))
    z = zh * 2 + zl
    feats, tokens = acts_ref.shape
    width = grad_ref.shape[-1]
    rank, depth = basis_ref.shape

    def ring(value, shift):
        return lax.rem(value + shift, 4)

    def line(shift):
        at = lax.rem(z + shift + 8, 8)
        return {"zh": at // 2, "zl": lax.rem(at, 2)}

    def remote(src, dst, send, recv, where):
        return pltpu.make_async_remote_copy(
            src_ref=src, dst_ref=dst, send_sem=send, recv_sem=recv, device_id=where, device_id_type=MESH
        )

    load_basis = pltpu.make_async_copy(basis_ref, basis_in, own_sem.at[3])
    load_start = pltpu.make_async_copy(start_ref, start_in, own_sem.at[4])
    save_scaled = pltpu.make_async_copy(basis_in, scaled_out, own_sem.at[5])
    save_grad = pltpu.make_async_copy(grad_ref, grad_out, own_sem.at[6])
    load_basis.start()
    load_start.start()

    barrier = pltpu.get_barrier_semaphore()
    greeted = 0
    for i in range(4):
        others = [{"zh": ring(zh, i), "y": ring(y, j)} for j in range(4) if i or j]
        others += [{"x": ring(x, i), "c": lax.rem(c + j, 2)} for j in range(2) if i or j]
        others += [{"zh": ring(zh, i), "zl": 1 - zl}]
        for where in others:
            pl.semaphore_signal(barrier, inc=1, device_id=where, device_id_type=MESH)
        greeted += len(others)
    pl.semaphore_wait(barrier, greeted)

    started = []

    def go(copy):
        copy.start()
        started.append(copy)

    def arrived(dst, sem):
        remote(dst, dst, sem, sem, {"x": ring(x, 1)}).wait_recv()

    def column(xx, cc):
        return pl.ds(pl.multiple_of((xx * 2 + cc) * width, width), width)

    mine = column(x, c)
    half = feats // 2

    def acts_piece(yy, shift):
        at = line(shift)
        return acts_all.at[yy, at["zh"], at["zl"]]

    def along_z(src, shift, hop):
        ways = []
        if shift <= 0:
            ways.append((0, 1, slice(0, half) if hop == 4 else slice(0, feats)))
        if shift >= 0:
            ways.append((1, -1, slice(half, feats) if hop == 4 else slice(0, feats)))
        for way, to, rows in ways:
            go(
                remote(
                    src.at[rows], acts_piece(y, shift).at[rows],
                    z_send.at[way, hop - 1], z_recv.at[way, hop - 1], line(to),
                )
            )

    def along_y(src, dst, shift):
        slot = shift + 3
        go(remote(src, dst, y_send.at[0, slot], y_recv.at[0, slot], {"y": ring(y, 1)}))
        go(remote(src, dst, y_send.at[1, slot], y_recv.at[1, slot], {"y": ring(y, 3)}))

    def acts_first(hop):
        if hop < 4:
            for way, shift in ((0, -hop), (1, hop)):
                piece = acts_piece(y, shift)
                arrived(piece, z_recv.at[way, hop - 1])
                along_z(piece, shift, hop + 1)
                along_y(piece, piece, shift)
        else:
            piece = acts_piece(y, 4)
            arrived(piece.at[slice(0, half)], z_recv.at[0, 3])
            arrived(piece.at[slice(half, feats)], z_recv.at[1, 3])
            along_y(piece, piece, 4)

    def acts_second(shift):
        slot = shift + 3
        up = slot % 2
        for k, back in enumerate((3, 1)):
            piece = acts_piece(ring(y, back), shift)
            arrived(piece, y_recv.at[k, slot])
            if k == up:
                go(remote(piece, piece, y_send.at[2, slot], y_recv.at[2, slot], {"y": ring(y, 4 - back)}))

    def acts_third(shift):
        arrived(acts_piece(ring(y, 2), shift), y_recv.at[2, shift + 3])

    def cotan_piece(to_zh, to_y):
        return cotan_ref.at[:, pl.ds(pl.multiple_of((to_zh * 4 + to_y) * width, width), width)]

    def cotan_direct(r, js=(1, 3, 2, 0)):
        for j in js:
            if r or j:
                to_zh, to_y = ring(zh, r), ring(y, j)
                go(
                    remote(
                        cotan_piece(to_zh, to_y), cotan_all.at[zh, y, :, mine],
                        d_send.at[r * 4 + j], d_recv.at[zh * 4 + y], {"zh": to_zh, "y": to_y},
                    )
                )

    def cotan_first(r):
        src = ring(zh, r)
        for j in range(4):
            if r or j:
                yy = ring(y, j)
                arrived(cotan_all.at[src, yy, :, mine], d_recv.at[src * 4 + yy])
            else:
                own_cotan.wait()
        block = cotan_all.at[src, :, :, mine]
        go(remote(block, block, x_send.at[0, r], x_recv.at[0, r], {"x": ring(x, 1)}))
        go(remote(block, block, x_send.at[1, r], x_recv.at[1, r], {"x": ring(x, 3)}))
        go(remote(block, block, c_send.at[0, r], c_recv.at[0, r], {"c": 1 - c}))

    def cotan_second(r):
        src = ring(zh, r)
        up = r // 2
        for k, back in enumerate((3, 1)):
            block = cotan_all.at[src, :, :, column(ring(x, back), c)]
            arrived(block, x_recv.at[k, r])
            if k == up:
                go(remote(block, block, x_send.at[2, r], x_recv.at[2, r], {"x": ring(x, 4 - back)}))
            go(remote(block, block, c_send.at[back, r], c_recv.at[back, r], {"c": 1 - c}))

    def cotan_third(r):
        block = cotan_all.at[ring(zh, r), :, :, column(ring(x, 2), c)]
        arrived(block, x_recv.at[2, r])
        go(remote(block, block, c_send.at[2, r], c_recv.at[2, r], {"c": 1 - c}))

    def multiply(r, begin, end):
        src = ring(zh, r)
        for shift in range(4):
            arrived(cotan_all.at[src, :, :, column(ring(x, shift), 1 - c)], c_recv.at[shift, r])

        def tile(n, carry):
            cut = pl.ds(pl.multiple_of(n * 256, 256), 256)
            part = jnp.zeros((2 * feats, 256), F32) if begin else total[:, cut]
            for j in range(4):
                left = acts_all[j, src].reshape(2 * feats, tokens)
                part += mm(left, cotan_all[src, j, :, cut], 1, 0)
            if end:
                sums[:, :, cut] = part.reshape(2, feats, 256).astype(BF)
            else:
                total[:, cut] = part
            return carry

        if not end:
            lax.fori_loop(0, 8 * width // 256, tile, 0)
            return
        for i in (2, 1, 3, 0):
            xx = ring(x, i)
            tile(xx, 0)
            for flip in (0, 1):
                if i or flip:
                    cc = lax.rem(c + flip, 2)
                    go(
                        remote(
                            sums.at[:, :, column(xx, cc)], grad_ref.at[:, x * 2 + c],
                            g_send.at[xx * 2 + cc], g_recv.at[x * 2 + c], {"x": xx, "c": cc},
                        )
                    )

    chunk, chunks = 512, depth // 512

    def prepare(begin, end):
        if begin == 0:
            load_basis.wait()
            load_start.wait()
            gram_bb[...] = jnp.zeros_like(gram_bb)
            coord_b[...] = jnp.zeros_like(coord_b)
        eye = lax.broadcasted_iota(jnp.int32, (rank, rank), 0) == lax.broadcasted_iota(
            jnp.int32, (rank, rank), 1
        )
        root = jnp.sqrt(jnp.sum(jnp.where(eye, values_ref[...], 0.0), axis=1, keepdims=True))

        def one(n, carry):
            cut = pl.ds(pl.multiple_of(n * chunk, chunk), chunk)
            scaled = (root * basis_in[:, cut].astype(F32)).astype(BF)
            basis_in[:, cut] = scaled
            gram_bb[...] += mm(scaled, scaled, 1, 1)
            coord_b[...] += mm(start_in[:, cut], scaled, 1, 1)
            return carry

        lax.fori_loop(begin, end, one, 0)
        if end == chunks:
            save_scaled.start()

    own_piece = acts_piece(y, 0)
    own_acts = pltpu.make_async_copy(acts_ref, own_piece, own_sem.at[0])
    own_cotan = pltpu.make_async_copy(cotan_piece(zh, y), cotan_all.at[zh, y, :, mine], own_sem.at[1])

    along_z(acts_ref, 0, 1)
    along_y(acts_ref, own_piece, 0)
    cotan_direct(0)
    own_acts.start()
    own_cotan.start()
    own_acts.wait()
    prepare(0, 3)
    acts_first(1)
    cotan_direct(1)
    cotan_direct(3)
    cotan_first(0)
    prepare(3, 6)
    acts_second(0)
    acts_first(2)
    cotan_second(0)
    prepare(6, 9)
    acts_second(1)
    acts_second(-1)
    cotan_direct(2, (1, 3))
    cotan_first(1)
    cotan_first(3)
    acts_first(3)
    cotan_direct(2, (2, 0))
    acts_second(2)
    acts_second(-2)
    cotan_third(0)
    cotan_second(1)
    cotan_second(3)
    acts_first(4)
    cotan_first(2)
    acts_second(3)
    acts_second(-3)
    acts_third(0)
    acts_third(1)
    acts_third(-1)
    multiply(0, True, False)
    acts_second(4)
    cotan_third(1)
    cotan_third(3)
    cotan_second(2)
    acts_third(2)
    acts_third(-2)
    acts_third(3)
    acts_third(-3)
    multiply(1, False, False)
    cotan_third(2)
    multiply(3, False, False)
    acts_third(4)
    multiply(2, False, True)

    own = pltpu.make_async_copy(sums.at[:, :, mine], grad_ref.at[:, x * 2 + c], own_sem.at[2])
    own.start()
    own.wait()
    for i in (0, 1, 3, 2):
        for flip in range(2):
            if i or flip:
                at = ring(x, i) * 2 + lax.rem(c + flip, 2)
                arrived(grad_ref.at[:, at], g_recv.at[at])
    save_grad.start()

    gram_bg = jnp.zeros((rank, width), F32)
    coord_g = jnp.zeros((rank, width), F32)
    gram_gg = jnp.zeros((width, width), F32)
    grad = grad_ref[...].reshape(depth, width)
    for at in range(0, depth, chunk):
        cut = slice(at, at + chunk)
        part = grad[cut]
        gram_bg += mm(basis_in[:, cut], part, 1, 0)
        coord_g += mm(start_in[:, cut], part, 1, 0)
        gram_gg += mm(part, part, 0, 0)
    gram_ref[:rank, :rank] = gram_bb[...]
    gram_ref[:rank, rank:] = gram_bg
    gram_ref[rank:, :rank] = gram_bg.T
    gram_ref[rank:, rank:] = gram_gg
    coords_ref[:, :rank] = coord_b[...].astype(BF)
    coords_ref[:, rank:] = coord_g.astype(BF)
    save_scaled.wait()
    save_grad.wait()
    for copy in started:
        copy.wait_send()


def gradient(acts, cotan, basis, values, start, width):
    feats, tokens = acts.shape
    rank, depth = basis.shape
    dma = pltpu.SemaphoreType.DMA
    anywhere = pl.BlockSpec(memory_space=pl.ANY)
    vmem = pl.BlockSpec(memory_space=pltpu.VMEM)
    return pl.pallas_call(
        gradient_kernel,
        out_shape=(
            jax.ShapeDtypeStruct((2, 8, feats, width), BF),
            jax.ShapeDtypeStruct((rank, depth), BF),
            jax.ShapeDtypeStruct((rank + width, rank + width), F32),
            jax.ShapeDtypeStruct((rank, rank + width), BF),
        ),
        in_specs=[anywhere, anywhere, anywhere, vmem, anywhere],
        out_specs=(anywhere, anywhere, vmem, vmem),
        scratch_shapes=[
            pltpu.VMEM((4, 4, 2, feats, tokens), BF),
            pltpu.VMEM((4, 4, tokens, 8 * width), BF),
            pltpu.VMEM((2 * feats, 8 * width), F32),
            pltpu.VMEM((2, feats, 8 * width), BF),
            pltpu.VMEM((2, 8, feats, width), BF),
            pltpu.VMEM((rank, depth), BF),
            pltpu.VMEM((rank, depth), BF),
            pltpu.VMEM((rank, rank), F32),
            pltpu.VMEM((rank, rank), F32),
            dma((7,)),
            dma((2, 4)), dma((2, 4)),
            dma((3, 8)), dma((3, 8)),
            dma((16,)), dma((16,)),
            dma((3, 4)), dma((3, 4)),
            dma((4, 4)), dma((4, 4)),
            dma((8,)), dma((8,)),
        ],
        compiler_params=pltpu.CompilerParams(
            collective_id=0, has_side_effects=True, vmem_limit_bytes=VMEM_LIMIT
        ),
    )(acts, cotan, basis, values, start)


def per_device(acts, cotan, sketch_basis, sketch_values, start_basis):
    shares = lax.axis_size("zh") * lax.axis_size("y")
    width = cotan.shape[1] // shares
    grad, scaled, gram, coords = gradient(
        acts.T, cotan, sketch_basis[0, 0], sketch_values[0], start_basis[0, 0], width
    )
    basis, values, update = sketch(grad.reshape(-1, width), scaled, gram, coords)
    update = exchange(update, shares)
    return basis[None, None], values[None], update


def solution(mesh):
    fine = jax.sharding.Mesh(mesh.devices.reshape(4, 4, 2, 4, 2), ("zh", "y", "zl", "x", "c"))
    dp, block = ("zh", "y"), ("zl", "x", "c")
    return jax.shard_map(
        per_device,
        mesh=fine,
        in_specs=(
            P(dp, block),
            P(dp, block),
            P(block, dp, None, None),
            P(block, dp, None),
            P(block, dp, None, None),
        ),
        out_specs=(P(block, dp, None, None), P(block, dp, None), P(dp, block)),
        check_vma=False,
    )
```

```python
import functools

import jax
import jax.numpy as jnp
from jax import lax
from jax.experimental import pallas as pl
from jax.experimental.pallas import tpu as pltpu
from jax.sharding import PartitionSpec as P

HIGH = lax.Precision.HIGHEST
F32, BF = jnp.float32, jnp.bfloat16
EPSILON = 1e-05
VMEM_LIMIT = 60 << 20
MESH = pl.DeviceIdType.MESH
PANEL = 8


def mm(a, b, ca, cb, precision=None):
    return lax.dot_general(
        a, b, (((ca,), (cb,)), ((), ())), precision=precision, preferred_element_type=F32
    )


def split(value, parts=3):
    out = []
    for _ in range(parts):
        out.append(value.astype(BF))
        value = value - out[-1].astype(F32)
    return out


def inverse_factor(block):
    n = block.shape[0]
    count = n // 8
    rows = [block[8 * i : 8 * i + 8, :] for i in range(count)]
    lane = lax.broadcasted_iota(jnp.int32, (8, n), 1)
    sub = lax.broadcasted_iota(jnp.int32, (8, n), 0)

    def full(v):
        return jnp.broadcast_to(v, (8, n))

    for start in range(0, n, PANEL):
        first = start // 8
        cols = [
            {i: full(rows[i][:, start + q : start + q + 1]) for i in range(first, count)}
            for q in range(PANEL)
        ]
        for q in range(PANEL):
            j = start + q
            b, r = divmod(j, 8)
            recip = 1.0 / full(cols[q][b][r : r + 1, :])
            mine = {i: cols[q][i] for i in range(b, count)}
            if r == 7:
                del mine[b]
            else:
                mine[b] = jnp.where(sub > r, mine[b], 0.0)
            mine = {i: m * recip for i, m in mine.items()}
            for k in range(q + 1, PANEL):
                pivot = full(cols[k][b][r : r + 1, :])
                for i, m in mine.items():
                    cols[k][i] = cols[k][i] - m * pivot
            here = lane == j
            row = jnp.where(here, 1.0, full(rows[b][r : r + 1, :]))
            for i, m in mine.items():
                gone = here & (sub > r) if i == b else here
                rows[i] = jnp.where(gone, 0.0, rows[i]) - m * row
    m = jnp.concatenate(rows, axis=0)
    ln = lax.broadcasted_iota(jnp.int32, (n, n), 1)
    sb = lax.broadcasted_iota(jnp.int32, (n, n), 0)
    diag = jnp.sum(jnp.where(ln == sb, m, 0.0), axis=1, keepdims=True)
    low = jnp.where(sb > ln, m, jnp.where(sb == ln, 1.0, 0.0))
    return low * lax.rsqrt(diag)


def solver(gram):
    h = gram.shape[0] // 2
    top = inverse_factor(gram[:h, :h])
    side = mm(gram[h:, :h], top, 1, 1, HIGH)
    low = inverse_factor(gram[h:, h:] - mm(side, side, 1, 1, HIGH))

    def solve(x):
        head = mm(top, x[:h], 1, 0, HIGH)
        tail = mm(low, x[h:] - mm(side, head, 1, 0, HIGH), 1, 0, HIGH)
        return jnp.concatenate([head, tail], axis=0)

    return solve


def sketch_kernel(
    grad_ref, scaled_ref, gram_ref, coords_ref, new_ref, energy_ref, update_ref, combine_ref, weights_ref
):
    rank = gram_ref.shape[0] - grad_ref.shape[1]

    @pl.when(pl.program_id(0) == 0)
    def _():
        combine, weights, energy_ref[...] = sketch_step(gram_ref[...], coords_ref[...], rank)
        for n, part in enumerate(combine):
            combine_ref[n] = part
        weights_ref[...] = weights

    step = 384
    for at in range(0, scaled_ref.shape[1], step):
        cut = slice(at, at + step)
        grad = grad_ref[cut, :]
        scaled = scaled_ref[:, cut]
        basis = sum(mm(combine_ref[n, :, :rank], scaled, 1, 0) for n in range(2))
        basis += sum(mm(combine_ref[n, :, rank:], grad, 1, 1) for n in range(2))
        basis = basis.astype(BF)
        new_ref[:, cut] = basis
        update_ref[cut, :] = (grad.astype(F32) + mm(basis, weights_ref[...], 0, 0)).astype(BF)


def sketch_step(gram, coords, rank):
    eye = lax.broadcasted_iota(jnp.int32, (rank, rank), 0) == lax.broadcasted_iota(
        jnp.int32, (rank, rank), 1
    )
    gram_parts = split(gram)

    def sweep(coords):
        mapped = sum(mm(coords, part, 1, 0) for part in gram_parts)
        images_gram = sum(mm(part, coords, 1, 1) for part in split(mapped))
        return mapped, solver(images_gram)

    mapped, solve = sweep(coords)
    coords = solve(mapped).astype(BF)
    mapped, solve = sweep(coords)
    total = coords.shape[1]
    solved = solve(jnp.concatenate([coords.astype(F32), mapped], axis=1))
    combine = split(solved[:, :total], 2)
    final = solved[:, total:]
    square = final * final
    energy = jnp.sum(square, axis=1, keepdims=True)
    lowest = jnp.min(energy)
    energy_row = jnp.sum(jnp.where(eye, energy, 0.0), axis=0, keepdims=True)
    shrink = jnp.sqrt(jnp.sqrt((lowest + EPSILON) / energy)) - 1.0
    weights = (shrink * final[:, rank:]).astype(BF)
    return combine, weights, energy_row - lowest


def sketch(grad, scaled, gram, coords):
    rank, depth = scaled.shape
    width = grad.shape[1]
    block = depth // 3
    return pl.pallas_call(
        sketch_kernel,
        grid=(depth // block,),
        out_shape=(
            jax.ShapeDtypeStruct((rank, depth), BF),
            jax.ShapeDtypeStruct((1, rank), F32),
            jax.ShapeDtypeStruct((depth, width), BF),
        ),
        in_specs=[
            pl.BlockSpec((block, width), lambda i: (i, 0)),
            pl.BlockSpec((rank, block), lambda i: (0, i)),
            pl.BlockSpec(gram.shape, lambda i: (0, 0)),
            pl.BlockSpec(coords.shape, lambda i: (0, 0)),
        ],
        out_specs=(
            pl.BlockSpec((rank, block), lambda i: (0, i)),
            pl.BlockSpec((1, rank), lambda i: (0, 0)),
            pl.BlockSpec((block, width), lambda i: (i, 0)),
        ),
        scratch_shapes=[
            pltpu.VMEM((2, rank, rank + width), BF),
            pltpu.VMEM((rank, width), BF),
        ],
        compiler_params=pltpu.CompilerParams(vmem_limit_bytes=VMEM_LIMIT),
    )(grad, scaled, gram, coords)


def exchange_kernel(shares, update_ref, out_ref, own_sem, send_sem, recv_sem):
    zh, y = lax.axis_index("zh"), lax.axis_index("y")
    ys = lax.axis_size("y")
    me = zh * ys + y
    rows, width = out_ref.shape[0], update_ref.shape[1]
    peers = [lax.rem(me + r, shares) for r in range(shares)]

    barrier = pltpu.get_barrier_semaphore()
    for peer in peers[1:]:
        pl.semaphore_signal(
            barrier, inc=1, device_id={"zh": peer // ys, "y": lax.rem(peer, ys)}, device_id_type=MESH
        )
    pl.semaphore_wait(barrier, shares - 1)

    columns = out_ref.at[:, pl.ds(pl.multiple_of(me * width, width), width)]

    def piece(peer):
        return update_ref.at[pl.ds(pl.multiple_of(peer * rows, 16), rows), :]

    copies = []
    for r in range(1, shares):
        peer = peers[r]
        copy = pltpu.make_async_remote_copy(
            src_ref=piece(peer),
            dst_ref=columns,
            send_sem=send_sem.at[r],
            recv_sem=recv_sem.at[r],
            device_id={"zh": peer // ys, "y": lax.rem(peer, ys)},
            device_id_type=MESH,
        )
        copy.start()
        copies.append(copy)
    own = pltpu.make_async_copy(piece(me), columns, own_sem)
    own.start()
    own.wait()
    for copy in copies:
        copy.wait()


def exchange(update, shares):
    depth, width = update.shape
    anywhere = pl.BlockSpec(memory_space=pl.ANY)
    return pl.pallas_call(
        functools.partial(exchange_kernel, shares),
        out_shape=jax.ShapeDtypeStruct((depth // shares, width * shares), BF),
        in_specs=[anywhere],
        out_specs=anywhere,
        scratch_shapes=[
            pltpu.SemaphoreType.DMA,
            pltpu.SemaphoreType.DMA((shares,)),
            pltpu.SemaphoreType.DMA((shares,)),
        ],
        compiler_params=pltpu.CompilerParams(
            collective_id=1, has_side_effects=True, vmem_limit_bytes=VMEM_LIMIT
        ),
    )(update)


def gradient_kernel(
    acts_ref, cotan_ref, basis_ref, values_ref, start_ref, grad_out, scaled_out, gram_ref, coords_ref,
    acts_all, cotan_all, total, sums, grad_ref, basis_in, start_in, gram_bb, coord_b,
    own_sem, z_send, z_recv, y_send, y_recv, d_send, d_recv, x_send, x_recv,
    c_send, c_recv, g_send, g_recv,
):
    zh, y, zl, x, c = (lax.axis_index(name) for name in ("zh", "y", "zl", "x", "c"))
    z = zh * 2 + zl
    feats, tokens = acts_ref.shape
    width = grad_ref.shape[-1]
    rank, depth = basis_ref.shape

    def ring(value, shift):
        return lax.rem(value + shift, 4)

    def line(shift):
        at = lax.rem(z + shift + 8, 8)
        return {"zh": at // 2, "zl": lax.rem(at, 2)}

    def remote(src, dst, send, recv, where):
        return pltpu.make_async_remote_copy(
            src_ref=src, dst_ref=dst, send_sem=send, recv_sem=recv, device_id=where, device_id_type=MESH
        )

    load_basis = pltpu.make_async_copy(basis_ref, basis_in, own_sem.at[3])
    load_start = pltpu.make_async_copy(start_ref, start_in, own_sem.at[4])
    save_scaled = pltpu.make_async_copy(basis_in, scaled_out, own_sem.at[5])
    save_grad = pltpu.make_async_copy(grad_ref, grad_out, own_sem.at[6])
    load_basis.start()
    load_start.start()

    barrier = pltpu.get_barrier_semaphore()
    greeted = 0
    for i in range(4):
        others = [{"zh": ring(zh, i), "y": ring(y, j)} for j in range(4) if i or j]
        others += [{"x": ring(x, i), "c": lax.rem(c + j, 2)} for j in range(2) if i or j]
        others += [{"zh": ring(zh, i), "zl": 1 - zl}]
        for where in others:
            pl.semaphore_signal(barrier, inc=1, device_id=where, device_id_type=MESH)
        greeted += len(others)
    pl.semaphore_wait(barrier, greeted)

    started = []

    def go(copy):
        copy.start()
        started.append(copy)

    def arrived(dst, sem):
        remote(dst, dst, sem, sem, {"x": ring(x, 1)}).wait_recv()

    def column(xx, cc):
        return pl.ds(pl.multiple_of((xx * 2 + cc) * width, width), width)

    mine = column(x, c)
    parts = (slice(0, 160), slice(160, feats))

    def acts_piece(yy, shift):
        at = line(shift)
        return acts_all.at[yy, at["zh"], at["zl"]]

    def along_z(src, shift, hop):
        ways = []
        if shift <= 0:
            ways.append((0, 1, parts[0] if hop == 4 else slice(0, feats)))
        if shift >= 0:
            ways.append((1, -1, parts[1] if hop == 4 else slice(0, feats)))
        for way, to, rows in ways:
            go(
                remote(
                    src.at[rows], acts_piece(y, shift).at[rows],
                    z_send.at[way, hop - 1], z_recv.at[way, hop - 1], line(to),
                )
            )

    def along_y(part, shift, src=None):
        dst = acts_piece(y, shift).at[parts[part]]
        src = dst if src is None else src.at[parts[part]]
        for k, to in enumerate((1, 3)):
            go(
                remote(
                    src, dst, y_send.at[k, part, shift + 3], y_recv.at[k, part, shift + 3], {"y": ring(y, to)}
                )
            )

    def acts_first(hop):
        if hop < 4:
            for way, shift in ((0, -hop), (1, hop)):
                piece = acts_piece(y, shift)
                arrived(piece, z_recv.at[way, hop - 1])
                along_z(piece, shift, hop + 1)
                along_y(0, shift)
        else:
            piece = acts_piece(y, 4)
            for way in range(2):
                arrived(piece.at[parts[way]], z_recv.at[way, 3])
                along_y(way, 4)

    def acts_second(part, shift):
        slot = shift + 3
        up = slot % 2
        for k, back in enumerate((3, 1)):
            piece = acts_piece(ring(y, back), shift).at[parts[part]]
            arrived(piece, y_recv.at[k, part, slot])
            if k == up:
                go(
                    remote(
                        piece, piece, y_send.at[2, part, slot], y_recv.at[2, part, slot],
                        {"y": ring(y, 4 - back)},
                    )
                )

    def acts_third(part, shift):
        arrived(acts_piece(ring(y, 2), shift).at[parts[part]], y_recv.at[2, part, shift + 3])

    def cotan_piece(to_zh, to_y):
        return cotan_ref.at[:, pl.ds(pl.multiple_of((to_zh * 4 + to_y) * width, width), width)]

    def cotan_direct(r, js=(1, 3, 2, 0)):
        for j in js:
            if r or j:
                to_zh, to_y = ring(zh, r), ring(y, j)
                go(
                    remote(
                        cotan_piece(to_zh, to_y), cotan_all.at[zh, lax.rem(y, 2), y // 2, :, mine],
                        d_send.at[r * 4 + j], d_recv.at[zh * 4 + y], {"zh": to_zh, "y": to_y},
                    )
                )

    def cotan_block(r, e, xx, cc):
        return cotan_all.at[ring(zh, r), lax.rem(y + 1 + e, 2), :, :, column(xx, cc)]

    def cotan_first(r, e):
        for j in ((1, 3), (2, 0))[e]:
            if r or j:
                src, yy = ring(zh, r), ring(y, j)
                arrived(cotan_all.at[src, lax.rem(yy, 2), yy // 2, :, mine], d_recv.at[src * 4 + yy])
            else:
                own_cotan.wait()
        n = 2 * r + e
        block = cotan_block(r, e, x, c)
        go(remote(block, block, x_send.at[0, n], x_recv.at[0, n], {"x": ring(x, 1)}))
        go(remote(block, block, x_send.at[1, n], x_recv.at[1, n], {"x": ring(x, 3)}))
        go(remote(block, block, c_send.at[0, n], c_recv.at[0, n], {"c": 1 - c}))

    def cotan_second(r, e):
        n = 2 * r + e
        for k, back in enumerate((3, 1)):
            block = cotan_block(r, e, ring(x, back), c)
            arrived(block, x_recv.at[k, n])
            if k == e:
                go(remote(block, block, x_send.at[2, n], x_recv.at[2, n], {"x": ring(x, 4 - back)}))
            go(remote(block, block, c_send.at[back, n], c_recv.at[back, n], {"c": 1 - c}))

    def cotan_third(r, e):
        n = 2 * r + e
        block = cotan_block(r, e, ring(x, 2), c)
        arrived(block, x_recv.at[2, n])
        go(remote(block, block, c_send.at[2, n], c_recv.at[2, n], {"c": 1 - c}))

    def cotan_last(r):
        for e in range(2):
            for shift in range(4):
                arrived(cotan_block(r, e, ring(x, shift), 1 - c), c_recv.at[shift, 2 * r + e])

    def multiply(r, part, begin, end):
        src = ring(zh, r)
        rows = parts[part]
        count = rows.stop - rows.start

        def tile(n, carry):
            cut = pl.ds(pl.multiple_of(n * 256, 256), 256)
            out = jnp.zeros((2 * count, 256), F32) if begin else total[:, rows, cut].reshape(2 * count, 256)
            for j in range(4):
                left = acts_all[j, src, :, rows].reshape(2 * count, tokens)
                out += mm(left, cotan_all[src, j % 2, j // 2, :, cut], 1, 0)
            out = out.reshape(2, count, 256)
            if end:
                sums[:, rows, cut] = out.astype(BF)
            else:
                total[:, rows, cut] = out
            return carry

        if not end:
            lax.fori_loop(0, 8 * width // 256, tile, 0)
            return
        for i in (2, 1, 3, 0):
            xx = ring(x, i)
            tile(xx, 0)
            for flip in (0, 1):
                if i or flip:
                    cc = lax.rem(c + flip, 2)
                    go(
                        remote(
                            sums.at[:, rows, column(xx, cc)], grad_ref.at[:, x * 2 + c, rows],
                            g_send.at[part, xx * 2 + cc], g_recv.at[part, x * 2 + c], {"x": xx, "c": cc},
                        )
                    )

    chunk, chunks = 512, depth // 512

    def prepare(begin, end):
        if begin == 0:
            load_basis.wait()
            load_start.wait()
            gram_bb[...] = jnp.zeros_like(gram_bb)
            coord_b[...] = jnp.zeros_like(coord_b)
        eye = lax.broadcasted_iota(jnp.int32, (rank, rank), 0) == lax.broadcasted_iota(
            jnp.int32, (rank, rank), 1
        )
        root = jnp.sqrt(jnp.sum(jnp.where(eye, values_ref[...], 0.0), axis=1, keepdims=True))

        def one(n, carry):
            cut = pl.ds(pl.multiple_of(n * chunk, chunk), chunk)
            scaled = (root * basis_in[:, cut].astype(F32)).astype(BF)
            basis_in[:, cut] = scaled
            gram_bb[...] += mm(scaled, scaled, 1, 1)
            coord_b[...] += mm(start_in[:, cut], scaled, 1, 1)
            return carry

        lax.fori_loop(begin, end, one, 0)
        if end == chunks:
            save_scaled.start()

    own_piece = acts_piece(y, 0)
    own_acts = pltpu.make_async_copy(acts_ref, own_piece, own_sem.at[0])
    own_cotan = pltpu.make_async_copy(cotan_piece(zh, y), cotan_all.at[zh, lax.rem(y, 2), y // 2, :, mine], own_sem.at[1])

    along_z(acts_ref, 0, 1)
    along_y(0, 0, acts_ref)
    along_y(1, 0, acts_ref)
    cotan_direct(0)
    own_acts.start()
    own_cotan.start()
    own_acts.wait()
    prepare(0, 3)
    prepare(3, 6)
    acts_first(1)
    cotan_direct(1)
    cotan_direct(3)
    cotan_first(0, 0)
    cotan_first(0, 1)
    along_y(1, 1)
    along_y(1, -1)
    acts_second(0, 0)
    acts_second(1, 0)
    acts_first(2)
    cotan_second(0, 0)
    cotan_second(0, 1)
    acts_second(0, 1)
    acts_second(0, -1)
    prepare(6, 9)
    cotan_direct(2)
    cotan_first(1, 0)
    cotan_first(3, 0)
    cotan_first(1, 1)
    cotan_first(3, 1)
    acts_first(3)
    acts_second(0, 2)
    acts_second(0, -2)
    cotan_third(0, 0)
    cotan_third(0, 1)
    acts_second(1, 1)
    acts_second(1, -1)
    cotan_second(1, 0)
    cotan_second(3, 0)
    cotan_second(1, 1)
    cotan_second(3, 1)
    along_y(1, 2)
    along_y(1, -2)
    acts_first(4)
    cotan_first(2, 0)
    acts_third(0, 0)
    acts_third(0, 1)
    acts_third(0, -1)
    cotan_last(0)
    multiply(0, 0, True, False)
    acts_second(0, 3)
    acts_second(0, -3)
    cotan_third(1, 0)
    cotan_third(3, 0)
    along_y(1, 3)
    along_y(1, -3)
    cotan_third(1, 1)
    cotan_third(3, 1)
    cotan_first(2, 1)
    cotan_second(2, 0)
    acts_second(0, 4)
    acts_second(1, 2)
    acts_second(1, -2)
    acts_third(1, 0)
    acts_third(1, 1)
    acts_third(1, -1)
    multiply(0, 1, True, False)
    cotan_second(2, 1)
    acts_third(0, 2)
    acts_third(0, -2)
    acts_third(0, 3)
    acts_third(0, -3)
    cotan_last(1)
    multiply(1, 0, False, False)
    cotan_last(3)
    multiply(3, 0, False, False)
    cotan_third(2, 0)
    acts_second(1, 3)
    acts_second(1, -3)
    acts_third(0, 4)
    cotan_third(2, 1)
    cotan_last(2)
    multiply(2, 0, False, True)
    acts_second(1, 4)
    acts_third(1, 2)
    acts_third(1, -2)
    acts_third(1, 3)
    acts_third(1, -3)
    multiply(1, 1, False, False)
    multiply(3, 1, False, False)
    acts_third(1, 4)
    multiply(2, 1, False, True)

    own = pltpu.make_async_copy(sums.at[:, :, mine], grad_ref.at[:, x * 2 + c], own_sem.at[2])
    own.start()
    own.wait()
    for part in range(2):
        for i in (0, 1, 3, 2):
            for flip in range(2):
                if i or flip:
                    at = ring(x, i) * 2 + lax.rem(c + flip, 2)
                    arrived(grad_ref.at[:, at, parts[part]], g_recv.at[part, at])
    save_grad.start()

    gram_bg = jnp.zeros((rank, width), F32)
    coord_g = jnp.zeros((rank, width), F32)
    gram_gg = jnp.zeros((width, width), F32)
    grad = grad_ref[...].reshape(depth, width)
    for at in range(0, depth, chunk):
        cut = slice(at, at + chunk)
        part = grad[cut]
        gram_bg += mm(basis_in[:, cut], part, 1, 0)
        coord_g += mm(start_in[:, cut], part, 1, 0)
        gram_gg += mm(part, part, 0, 0)
    gram_ref[:rank, :rank] = gram_bb[...]
    gram_ref[:rank, rank:] = gram_bg
    gram_ref[rank:, :rank] = gram_bg.T
    gram_ref[rank:, rank:] = gram_gg
    coords_ref[:, :rank] = coord_b[...].astype(BF)
    coords_ref[:, rank:] = coord_g.astype(BF)
    save_scaled.wait()
    save_grad.wait()
    for copy in started:
        copy.wait_send()


def gradient(acts, cotan, basis, values, start, width):
    feats, tokens = acts.shape
    rank, depth = basis.shape
    dma = pltpu.SemaphoreType.DMA
    anywhere = pl.BlockSpec(memory_space=pl.ANY)
    vmem = pl.BlockSpec(memory_space=pltpu.VMEM)
    return pl.pallas_call(
        gradient_kernel,
        out_shape=(
            jax.ShapeDtypeStruct((2, 8, feats, width), BF),
            jax.ShapeDtypeStruct((rank, depth), BF),
            jax.ShapeDtypeStruct((rank + width, rank + width), F32),
            jax.ShapeDtypeStruct((rank, rank + width), BF),
        ),
        in_specs=[anywhere, anywhere, anywhere, vmem, anywhere],
        out_specs=(anywhere, anywhere, vmem, vmem),
        scratch_shapes=[
            pltpu.VMEM((4, 4, 2, feats, tokens), BF),
            pltpu.VMEM((4, 2, 2, tokens, 8 * width), BF),
            pltpu.VMEM((2, feats, 8 * width), F32),
            pltpu.VMEM((2, feats, 8 * width), BF),
            pltpu.VMEM((2, 8, feats, width), BF),
            pltpu.VMEM((rank, depth), BF),
            pltpu.VMEM((rank, depth), BF),
            pltpu.VMEM((rank, rank), F32),
            pltpu.VMEM((rank, rank), F32),
            dma((7,)),
            dma((2, 4)), dma((2, 4)),
            dma((3, 2, 8)), dma((3, 2, 8)),
            dma((16,)), dma((16,)),
            dma((3, 8)), dma((3, 8)),
            dma((4, 8)), dma((4, 8)),
            dma((2, 8)), dma((2, 8)),
        ],
        compiler_params=pltpu.CompilerParams(
            collective_id=0, has_side_effects=True, vmem_limit_bytes=VMEM_LIMIT
        ),
    )(acts, cotan, basis, values, start)


def per_device(acts, cotan, sketch_basis, sketch_values, start_basis):
    shares = lax.axis_size("zh") * lax.axis_size("y")
    width = cotan.shape[1] // shares
    grad, scaled, gram, coords = gradient(
        acts.T, cotan, sketch_basis[0, 0], sketch_values[0], start_basis[0, 0], width
    )
    basis, values, update = sketch(grad.reshape(-1, width), scaled, gram, coords)
    update = exchange(update, shares)
    return basis[None, None], values[None], update


def solution(mesh):
    fine = jax.sharding.Mesh(mesh.devices.reshape(4, 4, 2, 4, 2), ("zh", "y", "zl", "x", "c"))
    dp, block = ("zh", "y"), ("zl", "x", "c")
    return jax.shard_map(
        per_device,
        mesh=fine,
        in_specs=(
            P(dp, block),
            P(dp, block),
            P(block, dp, None, None),
            P(block, dp, None),
            P(block, dp, None, None),
        ),
        out_specs=(P(block, dp, None, None), P(block, dp, None), P(dp, block)),
        check_vma=False,
    )
```

```python
import functools

import jax
import jax.numpy as jnp
from jax import lax
from jax.experimental import pallas as pl
from jax.experimental.pallas import tpu as pltpu
from jax.sharding import PartitionSpec as P

HIGH = lax.Precision.HIGHEST
F32, BF = jnp.float32, jnp.bfloat16
EPSILON = 1e-05
VMEM_LIMIT = 60 << 20
MESH = pl.DeviceIdType.MESH
PANEL = 8


def mm(a, b, ca, cb, precision=None):
    return lax.dot_general(
        a, b, (((ca,), (cb,)), ((), ())), precision=precision, preferred_element_type=F32
    )


def split(value, parts=3):
    out = []
    for _ in range(parts):
        out.append(value.astype(BF))
        value = value - out[-1].astype(F32)
    return out


def inverse_factor(block):
    n = block.shape[0]
    count = n // 8
    rows = [block[8 * i : 8 * i + 8, :] for i in range(count)]
    lane = lax.broadcasted_iota(jnp.int32, (8, n), 1)
    sub = lax.broadcasted_iota(jnp.int32, (8, n), 0)

    def full(v):
        return jnp.broadcast_to(v, (8, n))

    for start in range(0, n, PANEL):
        first = start // 8
        cols = [
            {i: full(rows[i][:, start + q : start + q + 1]) for i in range(first, count)}
            for q in range(PANEL)
        ]
        for q in range(PANEL):
            j = start + q
            b, r = divmod(j, 8)
            recip = 1.0 / full(cols[q][b][r : r + 1, :])
            mine = {i: cols[q][i] for i in range(b, count)}
            if r == 7:
                del mine[b]
            else:
                mine[b] = jnp.where(sub > r, mine[b], 0.0)
            mine = {i: m * recip for i, m in mine.items()}
            for k in range(q + 1, PANEL):
                pivot = full(cols[k][b][r : r + 1, :])
                for i, m in mine.items():
                    cols[k][i] = cols[k][i] - m * pivot
            here = lane == j
            row = jnp.where(here, 1.0, full(rows[b][r : r + 1, :]))
            for i, m in mine.items():
                gone = here & (sub > r) if i == b else here
                rows[i] = jnp.where(gone, 0.0, rows[i]) - m * row
    m = jnp.concatenate(rows, axis=0)
    ln = lax.broadcasted_iota(jnp.int32, (n, n), 1)
    sb = lax.broadcasted_iota(jnp.int32, (n, n), 0)
    diag = jnp.sum(jnp.where(ln == sb, m, 0.0), axis=1, keepdims=True)
    low = jnp.where(sb > ln, m, jnp.where(sb == ln, 1.0, 0.0))
    return low * lax.rsqrt(diag)


def solver(gram):
    h = gram.shape[0] // 2
    top = inverse_factor(gram[:h, :h])
    side = mm(gram[h:, :h], top, 1, 1, HIGH)
    low = inverse_factor(gram[h:, h:] - mm(side, side, 1, 1, HIGH))

    def solve(x):
        head = mm(top, x[:h], 1, 0, HIGH)
        tail = mm(low, x[h:] - mm(side, head, 1, 0, HIGH), 1, 0, HIGH)
        return jnp.concatenate([head, tail], axis=0)

    return solve


def sketch_kernel(
    grad_ref, scaled_ref, gram_ref, coords_ref, new_ref, energy_ref, update_ref, combine_ref, weights_ref
):
    rank = gram_ref.shape[0] - grad_ref.shape[1]

    @pl.when(pl.program_id(0) == 0)
    def _():
        combine, weights, energy_ref[...] = sketch_step(gram_ref[...], coords_ref[...], rank)
        for n, part in enumerate(combine):
            combine_ref[n] = part
        weights_ref[...] = weights

    step = 384
    for at in range(0, scaled_ref.shape[1], step):
        cut = slice(at, at + step)
        grad = grad_ref[cut, :]
        scaled = scaled_ref[:, cut]
        basis = sum(mm(combine_ref[n, :, :rank], scaled, 1, 0) for n in range(2))
        basis += sum(mm(combine_ref[n, :, rank:], grad, 1, 1) for n in range(2))
        basis = basis.astype(BF)
        new_ref[:, cut] = basis
        update_ref[cut, :] = (grad.astype(F32) + mm(basis, weights_ref[...], 0, 0)).astype(BF)


def sketch_step(gram, coords, rank):
    eye = lax.broadcasted_iota(jnp.int32, (rank, rank), 0) == lax.broadcasted_iota(
        jnp.int32, (rank, rank), 1
    )
    gram_parts = split(gram)

    def sweep(coords):
        mapped = sum(mm(coords, part, 1, 0) for part in gram_parts)
        images_gram = sum(mm(part, coords, 1, 1) for part in split(mapped))
        return mapped, solver(images_gram)

    mapped, solve = sweep(coords)
    coords = solve(mapped).astype(BF)
    mapped, solve = sweep(coords)
    total = coords.shape[1]
    solved = solve(jnp.concatenate([coords.astype(F32), mapped], axis=1))
    combine = split(solved[:, :total], 2)
    final = solved[:, total:]
    square = final * final
    energy = jnp.sum(square, axis=1, keepdims=True)
    lowest = jnp.min(energy)
    energy_row = jnp.sum(jnp.where(eye, energy, 0.0), axis=0, keepdims=True)
    shrink = jnp.sqrt(jnp.sqrt((lowest + EPSILON) / energy)) - 1.0
    weights = (shrink * final[:, rank:]).astype(BF)
    return combine, weights, energy_row - lowest


def sketch(grad, scaled, gram, coords):
    rank, depth = scaled.shape
    width = grad.shape[1]
    block = depth // 3
    return pl.pallas_call(
        sketch_kernel,
        grid=(depth // block,),
        out_shape=(
            jax.ShapeDtypeStruct((rank, depth), BF),
            jax.ShapeDtypeStruct((1, rank), F32),
            jax.ShapeDtypeStruct((depth, width), BF),
        ),
        in_specs=[
            pl.BlockSpec((block, width), lambda i: (i, 0)),
            pl.BlockSpec((rank, block), lambda i: (0, i)),
            pl.BlockSpec(gram.shape, lambda i: (0, 0)),
            pl.BlockSpec(coords.shape, lambda i: (0, 0)),
        ],
        out_specs=(
            pl.BlockSpec((rank, block), lambda i: (0, i)),
            pl.BlockSpec((1, rank), lambda i: (0, 0)),
            pl.BlockSpec((block, width), lambda i: (i, 0)),
        ),
        scratch_shapes=[
            pltpu.VMEM((2, rank, rank + width), BF),
            pltpu.VMEM((rank, width), BF),
        ],
        compiler_params=pltpu.CompilerParams(vmem_limit_bytes=VMEM_LIMIT),
    )(grad, scaled, gram, coords)


def exchange_kernel(shares, update_ref, out_ref, own_sem, send_sem, recv_sem):
    zh, y = lax.axis_index("zh"), lax.axis_index("y")
    ys = lax.axis_size("y")
    me = zh * ys + y
    rows, width = out_ref.shape[0], update_ref.shape[1]
    peers = [lax.rem(me + r, shares) for r in range(shares)]

    barrier = pltpu.get_barrier_semaphore()
    for peer in peers[1:]:
        pl.semaphore_signal(
            barrier, inc=1, device_id={"zh": peer // ys, "y": lax.rem(peer, ys)}, device_id_type=MESH
        )
    pl.semaphore_wait(barrier, shares - 1)

    columns = out_ref.at[:, pl.ds(pl.multiple_of(me * width, width), width)]

    def piece(peer):
        return update_ref.at[pl.ds(pl.multiple_of(peer * rows, 16), rows), :]

    copies = []
    for r in range(1, shares):
        peer = peers[r]
        copy = pltpu.make_async_remote_copy(
            src_ref=piece(peer),
            dst_ref=columns,
            send_sem=send_sem.at[r],
            recv_sem=recv_sem.at[r],
            device_id={"zh": peer // ys, "y": lax.rem(peer, ys)},
            device_id_type=MESH,
        )
        copy.start()
        copies.append(copy)
    own = pltpu.make_async_copy(piece(me), columns, own_sem)
    own.start()
    own.wait()
    for copy in copies:
        copy.wait()


def exchange(update, shares):
    depth, width = update.shape
    anywhere = pl.BlockSpec(memory_space=pl.ANY)
    return pl.pallas_call(
        functools.partial(exchange_kernel, shares),
        out_shape=jax.ShapeDtypeStruct((depth // shares, width * shares), BF),
        in_specs=[anywhere],
        out_specs=anywhere,
        scratch_shapes=[
            pltpu.SemaphoreType.DMA,
            pltpu.SemaphoreType.DMA((shares,)),
            pltpu.SemaphoreType.DMA((shares,)),
        ],
        compiler_params=pltpu.CompilerParams(
            collective_id=1, has_side_effects=True, vmem_limit_bytes=VMEM_LIMIT
        ),
    )(update)


def gradient_kernel(
    acts_ref, cotan_ref, basis_ref, values_ref, start_ref, grad_out, scaled_out, gram_ref, coords_ref,
    acts_all, cotan_all, total, sums, grad_ref, basis_in, start_in, gram_bb, coord_b,
    own_sem, z_send, z_recv, y_send, y_recv, d_send, d_recv, x_send, x_recv,
    c_send, c_recv, g_send, g_recv,
):
    zh, y, zl, x, c = (lax.axis_index(name) for name in ("zh", "y", "zl", "x", "c"))
    z = zh * 2 + zl
    feats, tokens = acts_ref.shape
    width = grad_ref.shape[-1]
    rank, depth = basis_ref.shape

    def ring(value, shift):
        return lax.rem(value + shift, 4)

    def line(shift):
        at = lax.rem(z + shift + 8, 8)
        return {"zh": at // 2, "zl": lax.rem(at, 2)}

    def remote(src, dst, send, recv, where):
        return pltpu.make_async_remote_copy(
            src_ref=src, dst_ref=dst, send_sem=send, recv_sem=recv, device_id=where, device_id_type=MESH
        )

    load_basis = pltpu.make_async_copy(basis_ref, basis_in, own_sem.at[3])
    load_start = pltpu.make_async_copy(start_ref, start_in, own_sem.at[4])
    save_scaled = pltpu.make_async_copy(basis_in, scaled_out, own_sem.at[5])
    save_grad = pltpu.make_async_copy(grad_ref, grad_out, own_sem.at[6])
    load_basis.start()
    load_start.start()

    barrier = pltpu.get_barrier_semaphore()
    greeted = 0
    for i in range(4):
        others = [{"zh": ring(zh, i), "y": ring(y, j)} for j in range(4) if i or j]
        others += [{"x": ring(x, i), "c": lax.rem(c + j, 2)} for j in range(2) if i or j]
        others += [{"zh": ring(zh, i), "zl": 1 - zl}]
        for where in others:
            pl.semaphore_signal(barrier, inc=1, device_id=where, device_id_type=MESH)
        greeted += len(others)
    pl.semaphore_wait(barrier, greeted)

    started = []

    def go(copy):
        copy.start()
        started.append(copy)

    def arrived(dst, sem):
        remote(dst, dst, sem, sem, {"x": ring(x, 1)}).wait_recv()

    def column(xx, cc):
        return pl.ds(pl.multiple_of((xx * 2 + cc) * width, width), width)

    mine = column(x, c)
    parts = (slice(0, 160), slice(160, feats))

    def acts_piece(yy, shift):
        at = line(shift)
        return acts_all.at[yy, at["zh"], at["zl"]]

    def along_z(src, shift, hop):
        ways = []
        if shift <= 0:
            ways.append((0, 1, parts[0] if hop == 4 else slice(0, feats)))
        if shift >= 0:
            ways.append((1, -1, parts[1] if hop == 4 else slice(0, feats)))
        for way, to, rows in ways:
            go(
                remote(
                    src.at[rows], acts_piece(y, shift).at[rows],
                    z_send.at[way, hop - 1], z_recv.at[way, hop - 1], line(to),
                )
            )

    def along_y(part, shift, src=None):
        dst = acts_piece(y, shift).at[parts[part]]
        src = dst if src is None else src.at[parts[part]]
        for k, to in enumerate((1, 3)):
            go(
                remote(
                    src, dst, y_send.at[k, part, shift + 3], y_recv.at[k, part, shift + 3], {"y": ring(y, to)}
                )
            )

    def acts_first(hop):
        if hop < 4:
            for way, shift in ((0, -hop), (1, hop)):
                piece = acts_piece(y, shift)
                arrived(piece, z_recv.at[way, hop - 1])
                along_z(piece, shift, hop + 1)
                along_y(0, shift)
        else:
            piece = acts_piece(y, 4)
            for way in range(2):
                arrived(piece.at[parts[way]], z_recv.at[way, 3])
                along_y(way, 4)

    def acts_second(part, shift):
        slot = shift + 3
        up = part if shift in (0, 4) else int(shift > 0)
        for k, back in enumerate((3, 1)):
            piece = acts_piece(ring(y, back), shift).at[parts[part]]
            arrived(piece, y_recv.at[k, part, slot])
            if k == up:
                go(
                    remote(
                        piece, piece, y_send.at[2, part, slot], y_recv.at[2, part, slot],
                        {"y": ring(y, 4 - back)},
                    )
                )

    def acts_third(part, shift):
        arrived(acts_piece(ring(y, 2), shift).at[parts[part]], y_recv.at[2, part, shift + 3])

    def cotan_piece(to_zh, to_y):
        return cotan_ref.at[:, pl.ds(pl.multiple_of((to_zh * 4 + to_y) * width, width), width)]

    def cotan_direct(r, js=(1, 3, 2, 0)):
        for j in js:
            if r or j:
                to_zh, to_y = ring(zh, r), ring(y, j)
                go(
                    remote(
                        cotan_piece(to_zh, to_y), cotan_all.at[zh, lax.rem(y, 2), y // 2, :, mine],
                        d_send.at[r * 4 + j], d_recv.at[zh * 4 + y], {"zh": to_zh, "y": to_y},
                    )
                )

    def cotan_block(r, e, xx, cc):
        return cotan_all.at[ring(zh, r), lax.rem(y + 1 + e, 2), :, :, column(xx, cc)]

    def cotan_first(r, e):
        for j in ((1, 3), (2, 0))[e]:
            if r or j:
                src, yy = ring(zh, r), ring(y, j)
                arrived(cotan_all.at[src, lax.rem(yy, 2), yy // 2, :, mine], d_recv.at[src * 4 + yy])
            else:
                own_cotan.wait()
        n = 2 * r + e
        block = cotan_block(r, e, x, c)
        go(remote(block, block, x_send.at[0, n], x_recv.at[0, n], {"x": ring(x, 1)}))
        go(remote(block, block, x_send.at[1, n], x_recv.at[1, n], {"x": ring(x, 3)}))
        go(remote(block, block, c_send.at[0, n], c_recv.at[0, n], {"c": 1 - c}))

    def cotan_second(r, e):
        n = 2 * r + e
        for k, back in enumerate((3, 1)):
            block = cotan_block(r, e, ring(x, back), c)
            arrived(block, x_recv.at[k, n])
            if k == e:
                go(remote(block, block, x_send.at[2, n], x_recv.at[2, n], {"x": ring(x, 4 - back)}))
            go(remote(block, block, c_send.at[back, n], c_recv.at[back, n], {"c": 1 - c}))

    def cotan_third(r, e):
        n = 2 * r + e
        block = cotan_block(r, e, ring(x, 2), c)
        arrived(block, x_recv.at[2, n])
        go(remote(block, block, c_send.at[2, n], c_recv.at[2, n], {"c": 1 - c}))

    def cotan_last(r):
        for e in range(2):
            for shift in range(4):
                arrived(cotan_block(r, e, ring(x, shift), 1 - c), c_recv.at[shift, 2 * r + e])

    def multiply(r, part, begin, end):
        src = ring(zh, r)
        rows = parts[part]
        count = rows.stop - rows.start

        def tile(n, carry):
            cut = pl.ds(pl.multiple_of(n * 256, 256), 256)
            out = jnp.zeros((2 * count, 256), F32) if begin else total[:, rows, cut].reshape(2 * count, 256)
            for j in range(4):
                left = acts_all[j, src, :, rows].reshape(2 * count, tokens)
                out += mm(left, cotan_all[src, j % 2, j // 2, :, cut], 1, 0)
            out = out.reshape(2, count, 256)
            if end:
                sums[:, rows, cut] = out.astype(BF)
            else:
                total[:, rows, cut] = out
            return carry

        if not end:
            lax.fori_loop(0, 8 * width // 256, tile, 0)
            return
        for i in (2, 1, 3, 0):
            xx = ring(x, i)
            tile(xx, 0)
            for flip in (0, 1):
                if i or flip:
                    cc = lax.rem(c + flip, 2)
                    go(
                        remote(
                            sums.at[:, rows, column(xx, cc)], grad_ref.at[:, x * 2 + c, rows],
                            g_send.at[part, xx * 2 + cc], g_recv.at[part, x * 2 + c], {"x": xx, "c": cc},
                        )
                    )

    chunk, chunks = 512, depth // 512

    def prepare(begin, end):
        if begin == 0:
            load_basis.wait()
            load_start.wait()
            gram_bb[...] = jnp.zeros_like(gram_bb)
            coord_b[...] = jnp.zeros_like(coord_b)
        eye = lax.broadcasted_iota(jnp.int32, (rank, rank), 0) == lax.broadcasted_iota(
            jnp.int32, (rank, rank), 1
        )
        root = jnp.sqrt(jnp.sum(jnp.where(eye, values_ref[...], 0.0), axis=1, keepdims=True))

        def one(n, carry):
            cut = pl.ds(pl.multiple_of(n * chunk, chunk), chunk)
            scaled = (root * basis_in[:, cut].astype(F32)).astype(BF)
            basis_in[:, cut] = scaled
            gram_bb[...] += mm(scaled, scaled, 1, 1)
            coord_b[...] += mm(start_in[:, cut], scaled, 1, 1)
            return carry

        lax.fori_loop(begin, end, one, 0)
        if end == chunks:
            save_scaled.start()

    own_piece = acts_piece(y, 0)
    own_acts = pltpu.make_async_copy(acts_ref, own_piece, own_sem.at[0])
    own_cotan = pltpu.make_async_copy(cotan_piece(zh, y), cotan_all.at[zh, lax.rem(y, 2), y // 2, :, mine], own_sem.at[1])

    along_z(acts_ref, 0, 1)
    along_y(0, 0, acts_ref)
    along_y(1, 0, acts_ref)
    cotan_direct(0)
    own_acts.start()
    own_cotan.start()
    own_acts.wait()
    prepare(0, 3)
    prepare(3, 6)
    acts_first(1)
    cotan_direct(1)
    cotan_direct(3)
    cotan_first(0, 0)
    cotan_first(0, 1)
    along_y(1, 1)
    along_y(1, -1)
    acts_second(0, 0)
    acts_second(1, 0)
    acts_first(2)
    cotan_second(0, 0)
    cotan_second(0, 1)
    acts_second(0, 1)
    acts_second(0, -1)
    prepare(6, 9)
    cotan_direct(2)
    cotan_first(1, 0)
    cotan_first(3, 0)
    cotan_first(1, 1)
    cotan_first(3, 1)
    acts_first(3)
    acts_second(0, 2)
    acts_second(0, -2)
    cotan_third(0, 0)
    cotan_third(0, 1)
    cotan_second(1, 0)
    cotan_second(3, 0)
    cotan_second(1, 1)
    cotan_second(3, 1)
    along_y(1, 2)
    along_y(1, -2)
    acts_first(4)
    cotan_first(2, 0)
    acts_second(1, 1)
    acts_second(1, -1)
    acts_third(0, 0)
    acts_third(0, 1)
    acts_third(0, -1)
    cotan_last(0)
    multiply(0, 0, True, False)
    acts_second(0, 3)
    acts_second(0, -3)
    cotan_third(1, 0)
    cotan_third(3, 0)
    along_y(1, 3)
    along_y(1, -3)
    cotan_first(2, 1)
    cotan_second(2, 0)
    cotan_third(1, 1)
    cotan_third(3, 1)
    acts_second(0, 4)
    cotan_second(2, 1)
    acts_second(1, 2)
    acts_second(1, -2)
    cotan_third(2, 0)
    acts_third(1, 0)
    acts_third(1, 1)
    acts_third(1, -1)
    multiply(0, 1, True, False)
    cotan_third(2, 1)
    acts_third(0, 2)
    acts_third(0, -2)
    acts_third(0, 3)
    acts_third(0, -3)
    cotan_last(1)
    multiply(1, 0, False, False)
    cotan_last(3)
    multiply(3, 0, False, False)
    acts_second(1, 3)
    acts_second(1, -3)
    acts_second(1, 4)
    acts_third(0, 4)
    cotan_last(2)
    multiply(2, 0, False, True)
    acts_third(1, 2)
    acts_third(1, -2)
    acts_third(1, 3)
    acts_third(1, -3)
    multiply(1, 1, False, False)
    multiply(3, 1, False, False)
    acts_third(1, 4)
    multiply(2, 1, False, True)

    own = pltpu.make_async_copy(sums.at[:, :, mine], grad_ref.at[:, x * 2 + c], own_sem.at[2])
    own.start()
    own.wait()
    for part in range(2):
        for i in (0, 1, 3, 2):
            for flip in range(2):
                if i or flip:
                    at = ring(x, i) * 2 + lax.rem(c + flip, 2)
                    arrived(grad_ref.at[:, at, parts[part]], g_recv.at[part, at])
    save_grad.start()

    gram_bg = jnp.zeros((rank, width), F32)
    coord_g = jnp.zeros((rank, width), F32)
    gram_gg = jnp.zeros((width, width), F32)
    grad = grad_ref[...].reshape(depth, width)
    for at in range(0, depth, chunk):
        cut = slice(at, at + chunk)
        part = grad[cut]
        gram_bg += mm(basis_in[:, cut], part, 1, 0)
        coord_g += mm(start_in[:, cut], part, 1, 0)
        gram_gg += mm(part, part, 0, 0)
    gram_ref[:rank, :rank] = gram_bb[...]
    gram_ref[:rank, rank:] = gram_bg
    gram_ref[rank:, :rank] = gram_bg.T
    gram_ref[rank:, rank:] = gram_gg
    coords_ref[:, :rank] = coord_b[...].astype(BF)
    coords_ref[:, rank:] = coord_g.astype(BF)
    save_scaled.wait()
    save_grad.wait()
    for copy in started:
        copy.wait_send()


def gradient(acts, cotan, basis, values, start, width):
    feats, tokens = acts.shape
    rank, depth = basis.shape
    dma = pltpu.SemaphoreType.DMA
    anywhere = pl.BlockSpec(memory_space=pl.ANY)
    vmem = pl.BlockSpec(memory_space=pltpu.VMEM)
    return pl.pallas_call(
        gradient_kernel,
        out_shape=(
            jax.ShapeDtypeStruct((2, 8, feats, width), BF),
            jax.ShapeDtypeStruct((rank, depth), BF),
            jax.ShapeDtypeStruct((rank + width, rank + width), F32),
            jax.ShapeDtypeStruct((rank, rank + width), BF),
        ),
        in_specs=[anywhere, anywhere, anywhere, vmem, anywhere],
        out_specs=(anywhere, anywhere, vmem, vmem),
        scratch_shapes=[
            pltpu.VMEM((4, 4, 2, feats, tokens), BF),
            pltpu.VMEM((4, 2, 2, tokens, 8 * width), BF),
            pltpu.VMEM((2, feats, 8 * width), F32),
            pltpu.VMEM((2, feats, 8 * width), BF),
            pltpu.VMEM((2, 8, feats, width), BF),
            pltpu.VMEM((rank, depth), BF),
            pltpu.VMEM((rank, depth), BF),
            pltpu.VMEM((rank, rank), F32),
            pltpu.VMEM((rank, rank), F32),
            dma((7,)),
            dma((2, 4)), dma((2, 4)),
            dma((3, 2, 8)), dma((3, 2, 8)),
            dma((16,)), dma((16,)),
            dma((3, 8)), dma((3, 8)),
            dma((4, 8)), dma((4, 8)),
            dma((2, 8)), dma((2, 8)),
        ],
        compiler_params=pltpu.CompilerParams(
            collective_id=0, has_side_effects=True, vmem_limit_bytes=VMEM_LIMIT
        ),
    )(acts, cotan, basis, values, start)


def per_device(acts, cotan, sketch_basis, sketch_values, start_basis):
    shares = lax.axis_size("zh") * lax.axis_size("y")
    width = cotan.shape[1] // shares
    grad, scaled, gram, coords = gradient(
        acts.T, cotan, sketch_basis[0, 0], sketch_values[0], start_basis[0, 0], width
    )
    basis, values, update = sketch(grad.reshape(-1, width), scaled, gram, coords)
    update = exchange(update, shares)
    return basis[None, None], values[None], update


def solution(mesh):
    fine = jax.sharding.Mesh(mesh.devices.reshape(4, 4, 2, 4, 2), ("zh", "y", "zl", "x", "c"))
    dp, block = ("zh", "y"), ("zl", "x", "c")
    return jax.shard_map(
        per_device,
        mesh=fine,
        in_specs=(
            P(dp, block),
            P(dp, block),
            P(block, dp, None, None),
            P(block, dp, None),
            P(block, dp, None, None),
        ),
        out_specs=(P(block, dp, None, None), P(block, dp, None), P(dp, block)),
        check_vma=False,
    )
```
